256 devices in a mesh: feat: 8 (over z), node: 32 (over x, y, core).
Axes of the slice: x: 4, y: 4, z: 8, core: 2. Of those that a mesh axis runs over, the one named last changes fastest.
Arguments:
- features: bfloat16 [32, 128, 8192], P('node', 'feat'), may hold values from -6 to 6
- tile_columns: int32 [32, 64, 8], P('node'), may hold values from 0 to 2047, as said below
- tile_count: int32 [32, 64], P('node'), may hold values from 1 to 8, as said below
- tile_bits: int32 [32, 64, 8, 2048], P('node'), may hold values from 0 to 255
- labels: int32 [32, 8192], P('node', 'feat'), may hold values from 0 to 171
- train_mask: int32 [32, 8192], P('node', 'feat'), may hold values from 0 to 1
- first_self: bfloat16 [128, 256], replicated, may hold values from -0.5 to 0.5
- first_neighbor: bfloat16 [128, 256], replicated, may hold values from -1.0546875 to 1.0546875
- first_bias: float32 [256], replicated, may hold values from -3 to 3
- second_self: bfloat16 [256, 172], replicated, may hold values from -1.125 to 1.125
- second_neighbor: bfloat16 [256, 172], replicated, may hold values from -1.125 to 1.125
- second_bias: float32 [172], replicated, may hold values from -4 to 4
Outputs:
- logits: float32 [32, 8192, 172], P('node', 'feat')
- loss: float32 [], replicated
- grad_self: float32 [256, 172], replicated
- grad_neighbor: float32 [256, 172], replicated
- grad_bias: float32 [172], replicated
The draws below stay inside these ranges and needn't reach their ends.
Inputs may be any that keep to these rules, and one draw needn't show every extreme that they name: `tile_columns`: column tiles are numbered over all 262144 nodes; every column tile of a row tile of block b lies in block b - 1, b or b + 1, and slot 0 of each row tile is the row tile itself. `tile_count`: slots at or after the count are ignored.
All inputs are finite; a program needn't handle non-finite values.
Results may differ from the reference program's by a relative error of at most 0.0008.
The reference program's roundings to bfloat16 on the way count: a program that leaves them out, or rounds other values in their place, can miss the bound.
Values may be sent and summed in bfloat16 or wider, within the bound.
A program may use at most 128 MiB of HBM per device.

```python
import math
import jax
import jax.numpy as jnp
from jax import lax

F_IN = 128
HID = 256
CLS = 172
DEG = 8
BLOCKS = 32
NB = 8192
TB = 64
NODES = 262144
NT = 2048


def draw_tile_columns(key, part):
    key = jax.random.fold_in(key, 11)
    block_total = NT // TB
    block_ids = jnp.arange(block_total, dtype=jnp.int32)[:, None, None]
    shape = (block_total, TB, DEG)
    lowest = jnp.broadcast_to(jnp.maximum(block_ids - 1, 0) * TB, shape)
    highest = jnp.broadcast_to(jnp.minimum(block_ids + 2, block_total) * TB, shape)
    columns = jax.random.randint(key, shape, lowest, highest, dtype=jnp.int32)
    diagonal = block_ids[:, :, 0] * TB + jnp.arange(TB, dtype=jnp.int32)[None, :]
    slot_ids = jnp.arange(DEG, dtype=jnp.int32)[None, None, :]
    return jnp.where(slot_ids == 0, diagonal[:, :, None], columns).astype(jnp.int32)


def draw_tile_count(key, part):
    key = jax.random.fold_in(key, 12)
    block_total = NT // TB
    busy_key, row_key = jax.random.split(key)
    busy = jax.random.randint(busy_key, (block_total, 1), 1, DEG + 1, dtype=jnp.int32)
    upper = jnp.broadcast_to(busy + 1, (block_total, TB))
    counts = jax.random.randint(row_key, (block_total, TB), 1, upper, dtype=jnp.int32)
    first_rows = jnp.arange(TB, dtype=jnp.int32)[None, :] == 0
    return jnp.where(first_rows, DEG, counts).astype(jnp.int32)


def draw_tile_bits(key, part):
    key = jax.random.fold_in(key, 13)
    shape = (NT // TB, TB, DEG, 128, 16)
    packed = jnp.zeros(shape, jnp.int32)
    for position in range(8):
        ones = (jax.random.randint(jax.random.fold_in(key, position), shape, 0, 32, dtype=jnp.int32) == 0).astype(jnp.int32)
        packed = packed + jnp.left_shift(ones, position)
    word_ids = jnp.arange(16, dtype=jnp.int32)[None, None, None, None, :]
    row_ids = jnp.arange(128, dtype=jnp.int32)[None, None, None, :, None]
    corner = (word_ids == 0) & (row_ids == 0)
    edge = (word_ids == 1) & (row_ids == 0)
    packed = jnp.where(corner, 255, packed)
    packed = jnp.where(edge, 0, packed)
    return packed.reshape(NT // TB, TB, DEG, 2048).astype(jnp.int32)


def draw_train_mask(key, part):
    key = jax.random.fold_in(key, 14)
    block_total = NT // TB
    node_ids = jnp.arange(NODES, dtype=jnp.int32).reshape(block_total, NB)
    tickets = jax.random.randint(key, (block_total, NB), 0, 4 * NODES, dtype=jnp.int32)
    return (tickets < NODES + 2 * node_ids).astype(jnp.int32)


def touch_ends(result, key, low, high):
    longest = result.shape.index(max(result.shape))
    spots = []
    for shift in (0, 1):
        where = [jax.random.randint(jax.random.fold_in(key, axis), (), 0, length) for axis, length in enumerate(result.shape)]
        where[longest] = (where[longest] + shift) % result.shape[longest]
        spots.append(tuple(where))
    return result.at[spots[0]].set(low).at[spots[1]].set(high)


def levels(rng, extent, shards, smallest, largest):
    def one(axis_at, blocks):
        heights = jax.random.uniform(jax.random.fold_in(jax.random.fold_in(rng, 6), axis_at), (blocks,), jnp.float32, smallest / len(shards), largest / len(shards))
        return jnp.repeat(jnp.exp(heights), extent[axis_at] // blocks).reshape((-1,) + (1,) * (len(extent) - axis_at - 1))

    level = one(*shards[0])
    for cut in shards[1:]:
        level = level * one(*cut)
    return level


def gaussian(stream_key, shape, deviation, limit, shards=(), held_as=jnp.bfloat16):
    entries = jax.random.normal(stream_key, shape, jnp.float32) * deviation
    if len(shards) > 0:
        entries = levels(stream_key, shape, shards, -0.22, 0.18) * entries
    return jnp.clip(entries, min=-limit, max=limit).astype(held_as)


def setup_inputs(seed: int = 0) -> dict:
    splits = jax.random.split(jax.random.key(seed), 13)
    return {
        "features": gaussian(splits[0], (BLOCKS, F_IN, NB), 1.0, 6.0, ((0, 32), (1, 8))),
        "tile_columns": draw_tile_columns(jax.random.fold_in(splits[12], 71), 0),
        "tile_count": draw_tile_count(jax.random.fold_in(splits[12], 71), 0),
        "tile_bits": draw_tile_bits(jax.random.fold_in(splits[12], 71), 0),
        "labels": touch_ends(jax.random.randint(splits[4], (BLOCKS, NB), 0, CLS), jax.random.fold_in(splits[4], 1), 0, CLS - 1).astype(jnp.int32),
        "train_mask": draw_train_mask(jax.random.fold_in(splits[12], 71), 0),
        "first_self": gaussian(splits[6], (F_IN, HID), F_IN ** -0.5, 0.5),
        "first_neighbor": gaussian(splits[7], (F_IN, HID), (2.0 * F_IN ** -0.5), 1.0546875),
        "first_bias": gaussian(splits[8], (HID,), 0.5, 3.0, (), jnp.float32),
        "second_self": gaussian(splits[9], (HID, CLS), (3.0 * HID ** -0.5), 1.125),
        "second_neighbor": gaussian(splits[10], (HID, CLS), (3.0 * HID ** -0.5), 1.125),
        "second_bias": gaussian(splits[11], (CLS,), 1.0, 4.0, (), jnp.float32),
    }


def unpack_bits(bit_words):
    shifts = jnp.arange(8, dtype=jnp.int32)
    rows = bit_words.reshape(bit_words.shape[:-1] + (128, 16))
    bit_table = jnp.bitwise_and(jnp.right_shift(rows[..., None], shifts), 1)
    return bit_table.reshape(rows.shape[:-1] + (128,))

def aggregate(table, columns, counts, bit_words):
    table_width = table.shape[-1]
    picked = jnp.take(table, columns, axis=0).astype(jnp.float32)
    slot_valid = (jnp.arange(columns.shape[1], dtype=jnp.int32)[None, :] < counts[:, None]).astype(jnp.int32)
    bit_table = unpack_bits(bit_words) * slot_valid[:, :, None, None]
    degree = lax.optimization_barrier(jnp.sum(bit_table, axis=(1, 3))).astype(jnp.float32)
    row_sums = jnp.einsum('tsij,tsjw->tiw', bit_table.astype(jnp.float32), picked)
    mean_rows = row_sums / jnp.maximum(degree, 1.0)[..., None]
    return mean_rows.reshape(-1, table_width).astype(jnp.bfloat16)

def reference(features, tile_columns, tile_count, tile_bits, labels, train_mask, first_self, first_neighbor, first_bias, second_self, second_neighbor, second_bias):
    node_major = jnp.transpose(features, (0, 2, 1))
    feature_tiles = node_major.reshape(-1, 128, node_major.shape[-1])

    def first_layer(block_data):
        own_rows, columns, counts, bit_words = block_data
        mean_rows = aggregate(feature_tiles, columns, counts, bit_words)
        preact = jnp.dot(own_rows, first_self, preferred_element_type=jnp.float32) + jnp.dot(mean_rows, first_neighbor, preferred_element_type=jnp.float32) + first_bias
        return jnp.maximum(preact, 0.0).astype(jnp.bfloat16)
    hidden = lax.map(first_layer, (node_major, tile_columns, tile_count, tile_bits))
    hidden_tiles = hidden.reshape(-1, 128, hidden.shape[-1])
    grad_scale = 1.0 / math.sqrt(NODES)

    def second_layer(block_data):
        own_rows, columns, counts, bit_words, class_ids, train_rows = block_data
        mean_rows = aggregate(hidden_tiles, columns, counts, bit_words)
        logits = jnp.dot(own_rows, second_self, preferred_element_type=jnp.float32) + jnp.dot(mean_rows, second_neighbor, preferred_element_type=jnp.float32) + second_bias
        exponent = jnp.exp(logits)
        class_total = lax.optimization_barrier(jnp.sum(exponent, axis=1))
        onehot = (jnp.arange(CLS, dtype=jnp.int32)[None, :] == class_ids[:, None]).astype(jnp.float32)
        weight = train_rows.astype(jnp.float32)
        row_loss = (jnp.log(class_total) - lax.optimization_barrier(jnp.sum(onehot * logits, axis=1))) * weight
        output_grad = ((exponent / class_total[:, None] - onehot) * weight[:, None] * grad_scale).astype(jnp.bfloat16)
        contract = (((0,), (0,)), ((), ()))
        grad_self = lax.dot_general(own_rows, output_grad, contract, preferred_element_type=jnp.float32)
        grad_neighbor = lax.dot_general(mean_rows, output_grad, contract, preferred_element_type=jnp.float32)
        grad_bias = lax.optimization_barrier(jnp.sum(output_grad.astype(jnp.float32), axis=0))
        return (logits, jnp.sum(row_loss), grad_self, grad_neighbor, grad_bias)
    logits, losses, self_parts, neighbor_parts, bias_parts = lax.map(second_layer, (hidden, tile_columns, tile_count, tile_bits, labels, train_mask))
    return (logits, jnp.sum(losses) / NODES, lax.optimization_barrier(jnp.sum(self_parts, axis=0)), lax.optimization_barrier(jnp.sum(neighbor_parts, axis=0)), lax.optimization_barrier(jnp.sum(bias_parts, axis=0)))
```

```python
import functools
import math

import jax
import jax.numpy as jnp
from jax import lax
from jax.experimental import pallas as pl
from jax.experimental.pallas import tpu as pltpu
from jax.sharding import PartitionSpec as P

MESH = pl.DeviceIdType.MESH
F32 = jnp.float32
BF16 = jnp.bfloat16
NT_DIMS = (((1,), (1,)), ((), ()))
LANES = 128
SLOTS = 8
BLOCK = 8192
TILES = 64
GROUPS = 8
GROUP = 1024
CLS = 172
CLS_PAD = 176
PIECE = 24
HALF = 384


def iota(shape, axis):
    return lax.broadcasted_iota(jnp.int32, shape, axis)


def lanes(index, width=LANES):
    return pl.ds(pl.multiple_of(index * width, width), width)


def rows(index, height):
    return pl.ds(pl.multiple_of(index * height, height), height)


def loop(low, high, body):
    def step(i, carry):
        body(i)
        return carry

    lax.fori_loop(low, high, step, 0)


def permutation():
    j, p = iota((LANES, LANES), 0), iota((LANES, LANES), 1)
    return (j == 8 * (p % 16) + p // 16).astype(F32).astype(BF16)


def exchange_bits(words):
    group = iota(words.shape, 1) // 16
    for level, low_bits in ((0, 0x55555555), (1, 0x33333333), (2, 0x0F0F0F0F)):
        distance = 1 << level
        upper = ((group >> level) & 1) == 1
        keep = jnp.where(upper, ~jnp.int32(low_bits), jnp.int32(low_bits))
        from_above = pltpu.roll(words, LANES - 16 * distance, 1) << distance
        from_below = pltpu.roll(words, 16 * distance, 1) >> distance
        words = (words & keep) | (jnp.where(upper, from_below, from_above) & ~keep)
    return words


def unpack_row_tile(t, count_ref, bits, adj):
    limit = jnp.full((8, LANES), count_ref[0, t], jnp.int32)
    for pair in range(SLOTS // 2):
        packed = None
        for part in range(4):
            slot, half = 2 * pair + part // 2, part % 2
            piece = bits[t, pl.ds(64 * half + slot, 8, stride=8), :]
            piece = jnp.where(limit > slot, piece, 0) << (8 * part)
            packed = piece if packed is None else packed | piece
        packed = exchange_bits(packed)
        for side in range(2):
            slot = 2 * pair + side
            for low in range(8):
                first = (packed >> (16 * side + low)) & 1
                second = (packed >> (16 * side + 8 + low)) & 1
                both = jnp.concatenate([first, second], axis=0).astype(F32).astype(BF16)
                adj[t, 16 * low : 16 * low + 16, LANES * slot : LANES * (slot + 1)] = both


def picked_tiles(t, first_column, column_ref, table):
    parts = []
    for slot in range(SLOTS):
        index = jnp.clip(column_ref[t, slot] - first_column, 0, 3 * TILES - 1)
        parts.append(table[index])
    return jnp.concatenate(parts, axis=1)


def kernel(
    scale,
    features,
    column_ref,
    count_ref,
    bit_words,
    labels,
    train_mask,
    first_self,
    first_neighbor,
    first_bias,
    second_self,
    second_neighbor,
    second_bias,
    logits_out,
    total_out,
    feats,
    bits,
    adj,
    table1,
    stage1,
    inputs1,
    table2,
    stage2,
    parts1,
    parts2,
    hidden,
    mean2,
    inv_degree,
    w1,
    w2,
    b1,
    b2,
    class_mask,
    logits,
    logits_rows,
    turn_left,
    turn_right,
    grad,
    payload,
    core_in,
    half_sum,
    plane_in,
    line_in,
    total,
    bit_sem,
    local_sem,
    halo1_send,
    halo1_recv,
    x_send,
    x_recv,
    m_send,
    m_recv,
    h_send,
    h_recv,
    halo2_send,
    halo2_recv,
    n_send,
    n_recv,
    core_send,
    core_recv,
    plane_send,
    plane_recv,
    line_send,
    line_recv,
    back_send,
    back_recv,
):
    z = lax.axis_index("feat")
    node = lax.axis_index("node")
    core = lax.rem(node, 2)
    plane = lax.div(node, 2)
    up = lax.rem(node + 1, 32)
    down = lax.rem(node + 31, 32)
    core_peer = plane * 2 + 1 - core
    first_column = (node - 1) * TILES

    def around(offset):
        return lax.rem(z + offset, GROUPS)

    def plane_peer(offset):
        return lax.rem(plane + offset, 16)

    def send(src, dst, send_sem, recv_sem, device):
        return pltpu.make_async_remote_copy(
            src_ref=src,
            dst_ref=dst,
            send_sem=send_sem,
            recv_sem=recv_sem,
            device_id=device,
            device_id_type=MESH,
        )

    barrier = pltpu.get_barrier_semaphore()

    def greet(device):
        pl.semaphore_signal(barrier, inc=1, device_id=device, device_id_type=MESH)

    loop(1, GROUPS, lambda o: greet((around(o), node)))
    loop(1, 16, lambda o: greet((z, plane_peer(o) * 2 + core)))
    greet((z, up))
    greet((z, down))

    feature_copy = pltpu.make_async_copy(features.at[0], feats, local_sem.at[0])
    feature_copy.start()

    def bit_copy(r):
        return pltpu.make_async_copy(
            bit_words.at[0, :, :, lanes(r)], bits.at[:, rows(r, 8), :], bit_sem.at[r]
        )

    loop(0, 16, lambda r: bit_copy(r).start())

    perm = permutation()
    feature_copy.wait()

    def permute_features(t):
        moved = jnp.dot(feats[:, lanes(t)], perm, preferred_element_type=F32)
        table1[TILES + t] = moved.astype(BF16)

    loop(0, TILES, permute_features)
    pl.semaphore_wait(barrier, 24)

    own1 = table1.at[pl.ds(TILES, TILES)]
    to_up1 = send(own1, table1.at[pl.ds(0, TILES)], halo1_send.at[0], halo1_recv.at[0], (z, up))
    to_down1 = send(own1, table1.at[pl.ds(2 * TILES, TILES)], halo1_send.at[1], halo1_recv.at[1], (z, down))
    to_up1.start()
    to_down1.start()

    def send_x(group, source):
        return send(
            table1.at[pl.ds(TILES + 8 * group, 8)],
            inputs1.at[source],
            x_send.at[group],
            x_recv.at[source],
            (group, node),
        )

    def send_m(group, source):
        return send(
            stage1.at[pl.ds(8 * group, 8)],
            inputs1.at[8 + source],
            m_send.at[group],
            m_recv.at[source],
            (group, node),
        )

    def send_h(group, source):
        return send(
            parts1.at[group],
            table2.at[pl.ds(TILES + 8 * source, 8)],
            h_send.at[group],
            h_recv.at[source],
            (group, node),
        )

    def send_n(group, source):
        return send(
            stage2.at[pl.ds(8 * group, 8)],
            parts2.at[source],
            n_send.at[group],
            n_recv.at[source],
            (group, node),
        )

    loop(1, GROUPS, lambda o: send_x(around(o), z).start())
    x_own = pltpu.make_async_copy(
        table1.at[pl.ds(TILES + 8 * z, 8)], inputs1.at[z], local_sem.at[1]
    )
    x_own.start()

    eye = (iota((256, 256), 0) == iota((256, 256), 1)).astype(F32).astype(BF16)
    for part, weight in enumerate((first_self, first_neighbor)):
        turned = lax.dot_general(eye, weight[...], NT_DIMS, preferred_element_type=F32)
        w1[:, LANES * part : LANES * (part + 1)] = turned.astype(BF16)
    pick = (iota((CLS_PAD, CLS), 0) == iota((CLS_PAD, CLS), 1)).astype(F32)
    for part, weight in enumerate((second_self, second_neighbor)):
        turned = lax.dot_general(pick.astype(BF16), weight[...], NT_DIMS, preferred_element_type=F32)
        w2[:, 256 * part : 256 * (part + 1)] = turned.astype(BF16)
    column1 = jnp.sum(
        jnp.where(iota((256, 256), 0) == iota((256, 256), 1), first_bias[...], 0.0),
        axis=1,
        keepdims=True,
    )
    b1[...] = jnp.broadcast_to(column1, (256, LANES))
    column2 = jnp.sum(jnp.where(pick > 0.5, second_bias[...], 0.0), axis=1, keepdims=True)
    column2 = jnp.where(iota((CLS_PAD, 1), 0) < CLS, column2, -1e30)
    b2[...] = jnp.broadcast_to(column2, (CLS_PAD, LANES))
    both = jnp.where(
        iota((16, GROUP), 0) < 8,
        jnp.broadcast_to(labels[...].astype(F32), (16, GROUP)),
        jnp.broadcast_to(train_mask[...].astype(F32), (16, GROUP)),
    ).astype(BF16)
    for u in range(8):
        span = slice(LANES * u, LANES * (u + 1))
        class_mask[:, span] = jnp.dot(both[:, span], perm, preferred_element_type=F32)

    loop(0, 16, lambda r: bit_copy(r).wait())
    loop(0, TILES, lambda t: unpack_row_tile(t, count_ref, bits, adj))

    to_up1.wait_recv()
    to_down1.wait_recv()

    def first_tile(t):
        values = picked_tiles(t, first_column, column_ref, table1)
        stacked = jnp.concatenate([values, jnp.ones((16, SLOTS * LANES), BF16)], axis=0)
        sums = lax.dot_general(stacked, adj[t], NT_DIMS, preferred_element_type=F32)
        inverse = 1.0 / jnp.maximum(sums[16:24], 1.0)
        inv_degree[t] = inverse
        stage1[t] = (sums[:16] * inverse[:1]).astype(BF16)

    def first_group(o):
        group = around(o)
        loop(0, 8, lambda u: first_tile(group * 8 + u))

        @pl.when(o < GROUPS)
        def _():
            send_m(group, z).start()

    loop(1, GROUPS + 1, first_group)
    m_own = pltpu.make_async_copy(
        stage1.at[pl.ds(8 * z, 8)], inputs1.at[8 + z], local_sem.at[2]
    )
    m_own.start()
    x_own.wait()
    m_own.wait()
    loop(1, GROUPS, lambda o: send_x(z, around(o)).wait_recv())
    loop(1, GROUPS, lambda o: send_m(z, around(o)).wait_recv())

    def first_dense(u):
        node_inputs = inputs1[:, u].reshape(256, LANES)
        total1 = jnp.dot(w1[...], node_inputs, preferred_element_type=F32)
        activated = jnp.maximum(total1 + b1[...], 0.0).astype(BF16)
        hidden[:, lanes(u)] = activated
        parts1[:, u] = activated.reshape(GROUPS, 32, LANES)

    loop(0, 8, first_dense)
    loop(1, GROUPS, lambda o: send_h(around(o), z).start())
    table2[pl.ds(TILES + 8 * z, 8)] = parts1[z]

    def halo2(group, side, device):
        return send(
            table2.at[pl.ds(TILES + 8 * group, 8)],
            table2.at[pl.ds(2 * TILES * side + 8 * group, 8)],
            halo2_send.at[side, group],
            halo2_recv.at[side, group],
            (z, device),
        )

    def forward(group):
        halo2(group, 0, up).start()
        halo2(group, 1, down).start()

    forward(z)

    def pass_on(o):
        group = around(o)
        send_h(z, group).wait_recv()
        forward(group)

    loop(1, GROUPS, pass_on)

    def halo2_arrived(group):
        halo2(group, 0, up).wait_recv()
        halo2(group, 1, down).wait_recv()

    loop(0, GROUPS, halo2_arrived)

    def second_tile(t):
        values = picked_tiles(t, first_column, column_ref, table2)
        sums = lax.dot_general(values, adj[t], NT_DIMS, preferred_element_type=F32)
        stage2[t] = (sums * inv_degree[t][:1]).astype(BF16)

    def second_group(o):
        group = around(o)
        loop(0, 8, lambda u: second_tile(group * 8 + u))

        @pl.when(o < GROUPS)
        def _():
            send_n(group, z).start()

    loop(1, GROUPS + 1, second_group)
    parts2[z] = stage2[pl.ds(8 * z, 8)]
    loop(1, GROUPS, lambda o: send_n(z, around(o)).wait_recv())

    def second_dense(u, loss):
        span = lanes(u)
        mean2[:, span] = parts2[:, u].reshape(256, LANES)
        score = (
            jnp.dot(w2[:, :256], hidden[:, span], preferred_element_type=F32)
            + jnp.dot(w2[:, 256:], mean2[:, span], preferred_element_type=F32)
            + b2[...]
        )
        logits[:, span] = score
        exponent = jnp.exp(score)
        class_total = jnp.sum(exponent, axis=0, keepdims=True)
        label = class_mask[0:1, span].astype(jnp.int32)
        weight = class_mask[8:9, span]
        chosen = iota((CLS_PAD, LANES), 0) == label
        own_score = jnp.sum(jnp.where(chosen, score, 0.0), axis=0, keepdims=True)
        slope = exponent * (1.0 / class_total) - jnp.where(chosen, 1.0, 0.0)
        grad[0:CLS_PAD, span] = (slope * (weight * scale)).astype(BF16)
        return loss + (jnp.log(class_total) - own_score) * weight

    grad[CLS_PAD:256, :] = jnp.zeros((256 - CLS_PAD, GROUP), BF16)
    loss_lanes = lax.fori_loop(0, 8, second_dense, jnp.zeros((1, LANES), F32))
    loss = jnp.sum(loss_lanes, axis=1, keepdims=True) * (scale * scale)
    bias = jnp.sum(grad[...].astype(F32), axis=1, keepdims=True)
    payload[0:256] = lax.dot_general(hidden[...], grad[0:128], NT_DIMS, preferred_element_type=F32)
    payload[256:512] = lax.dot_general(mean2[...], grad[0:128], NT_DIMS, preferred_element_type=F32)
    tail = grad[128:256]
    tail_self = lax.dot_general(hidden[...], tail, NT_DIMS, preferred_element_type=F32)
    tail_neighbor = lax.dot_general(mean2[...], tail, NT_DIMS, preferred_element_type=F32)
    last = iota((256, LANES), 1) == 127
    extra = jnp.where(iota((256, LANES), 0) == 200, loss, bias)
    payload[512:768] = jnp.where(last, extra, tail_self + pltpu.roll(tail_neighbor, 64, 1))

    core_copy = send(
        payload.at[rows(1 - core, HALF), :], core_in, core_send.at[0], core_recv.at[0], (z, core_peer)
    )
    core_copy.start()

    def turn(u):
        turned = logits[:, lanes(u)].T
        for low in range(8):
            place = pl.ds(low, 16, stride=8)
            turn_left[place, :] = turned[16 * low : 16 * low + 16, :LANES]
            turn_right[place, : CLS_PAD - LANES] = turned[16 * low : 16 * low + 16, LANES:]
        logits_rows[rows(u, LANES), :LANES] = turn_left[...]
        logits_rows[rows(u, LANES), LANES:] = turn_right[:, : CLS - LANES]

    loop(0, 8, turn)
    logits_copy = pltpu.make_async_copy(logits_rows, logits_out.at[0], local_sem.at[3])
    logits_copy.start()

    core_copy.wait_recv()
    half_sum[...] = payload[rows(core, HALF), :] + core_in[...]

    def plane_copy(target, source):
        return send(
            half_sum.at[rows(target, PIECE), :],
            plane_in.at[source],
            plane_send.at[target],
            plane_recv.at[source],
            (z, target * 2 + core),
        )

    loop(1, 16, lambda o: plane_copy(plane_peer(o), plane).start())
    plane_in[plane] = half_sum[rows(plane, PIECE), :]
    loop(1, 16, lambda o: plane_copy(plane, plane_peer(o)).wait_recv())
    line_in[z] = jnp.sum(plane_in[...], axis=0)

    def line_copy(target, source):
        return send(
            line_in.at[source], line_in.at[source], line_send.at[target], line_recv.at[source], (target, node)
        )

    loop(1, GROUPS, lambda o: line_copy(around(o), z).start())
    loop(1, GROUPS, lambda o: line_copy(z, around(o)).wait_recv())
    total[rows(core * 16 + plane, PIECE), :] = jnp.sum(line_in[...], axis=0)

    def back_copy(target, source):
        part = total.at[rows(core * 16 + source, PIECE), :]
        return send(part, part, back_send.at[target], back_recv.at[source], (z, target * 2 + core))

    loop(1, 16, lambda o: back_copy(plane_peer(o), plane).start())
    loop(1, 16, lambda o: back_copy(plane, plane_peer(o)).wait_recv())

    def half_copy(which):
        part = total.at[rows(which, HALF), :]
        return send(part, part, core_send.at[1], core_recv.at[1], (z, core_peer))

    half_copy(core).start()
    half_copy(1 - core).wait_recv()
    result = pltpu.make_async_copy(total, total_out, local_sem.at[4])
    result.start()

    to_up1.wait_send()
    to_down1.wait_send()

    def left_line(o):
        group = around(o)
        send_x(group, z).wait_send()
        send_m(group, z).wait_send()
        send_h(group, z).wait_send()
        send_n(group, z).wait_send()
        line_copy(group, z).wait_send()

    loop(1, GROUPS, left_line)

    def left_halo(group):
        halo2(group, 0, up).wait_send()
        halo2(group, 1, down).wait_send()

    loop(0, GROUPS, left_halo)

    def left_plane(o):
        target = plane_peer(o)
        plane_copy(target, plane).wait_send()
        back_copy(target, plane).wait_send()

    loop(1, 16, left_plane)
    core_copy.wait_send()
    half_copy(core).wait_send()
    logits_copy.wait()
    result.wait()


def shards(
    features,
    tile_columns,
    tile_count,
    tile_bits,
    labels,
    train_mask,
    first_self,
    first_neighbor,
    first_bias,
    second_self,
    second_neighbor,
    second_bias,
):
    node_total = features.shape[2] * lax.axis_size("node")
    dma = pltpu.SemaphoreType.DMA
    vmem = pl.BlockSpec(memory_space=pltpu.VMEM)
    smem = pl.BlockSpec(memory_space=pltpu.SMEM)
    anywhere = pl.BlockSpec(memory_space=pl.ANY)
    logits, total = pl.pallas_call(
        functools.partial(kernel, 1.0 / math.sqrt(node_total)),
        out_shape=(
            jax.ShapeDtypeStruct((1, GROUP, CLS), F32),
            jax.ShapeDtypeStruct((2 * HALF, LANES), F32),
        ),
        in_specs=[anywhere, smem, smem, anywhere] + [vmem] * 8,
        out_specs=(anywhere, anywhere),
        scratch_shapes=[
            pltpu.VMEM((16, BLOCK), BF16),
            pltpu.VMEM((TILES, 128, LANES), jnp.int32),
            pltpu.VMEM((TILES, LANES, SLOTS * LANES), BF16),
            pltpu.VMEM((3 * TILES, 16, LANES), BF16),
            pltpu.VMEM((TILES, 16, LANES), BF16),
            pltpu.VMEM((2 * GROUPS, 8, 16, LANES), BF16),
            pltpu.VMEM((3 * TILES, 32, LANES), BF16),
            pltpu.VMEM((TILES, 32, LANES), BF16),
            pltpu.VMEM((GROUPS, 8, 32, LANES), BF16),
            pltpu.VMEM((GROUPS, 8, 32, LANES), BF16),
            pltpu.VMEM((256, GROUP), BF16),
            pltpu.VMEM((256, GROUP), BF16),
            pltpu.VMEM((TILES, 8, LANES), F32),
            pltpu.VMEM((256, 256), BF16),
            pltpu.VMEM((CLS_PAD, 512), BF16),
            pltpu.VMEM((256, LANES), F32),
            pltpu.VMEM((CLS_PAD, LANES), F32),
            pltpu.VMEM((16, GROUP), F32),
            pltpu.VMEM((CLS_PAD, GROUP), F32),
            pltpu.VMEM((GROUP, CLS), F32),
            pltpu.VMEM((LANES, LANES), F32),
            pltpu.VMEM((LANES, LANES), F32),
            pltpu.VMEM((256, GROUP), BF16),
            pltpu.VMEM((2 * HALF, LANES), F32),
            pltpu.VMEM((HALF, LANES), F32),
            pltpu.VMEM((HALF, LANES), F32),
            pltpu.VMEM((16, PIECE, LANES), F32),
            pltpu.VMEM((GROUPS, PIECE, LANES), F32),
            pltpu.VMEM((2 * HALF, LANES), F32),
            dma((16,)),
            dma((5,)),
            dma((2,)),
            dma((2,)),
            dma((GROUPS,)),
            dma((GROUPS,)),
            dma((GROUPS,)),
            dma((GROUPS,)),
            dma((GROUPS,)),
            dma((GROUPS,)),
            dma((2, GROUPS)),
            dma((2, GROUPS)),
            dma((GROUPS,)),
            dma((GROUPS,)),
            dma((2,)),
            dma((2,)),
            dma((16,)),
            dma((16,)),
            dma((GROUPS,)),
            dma((GROUPS,)),
            dma((16,)),
            dma((16,)),
        ],
        compiler_params=pltpu.CompilerParams(
            collective_id=0, has_side_effects=True, vmem_limit_bytes=52 * 1024 * 1024
        ),
    )(
        features,
        tile_columns[0],
        tile_count,
        tile_bits,
        labels,
        train_mask,
        first_self,
        first_neighbor,
        first_bias[None],
        second_self,
        second_neighbor,
        second_bias[None],
    )
    tail = total[512:]
    grad_self = jnp.concatenate([total[:256], tail[:, : CLS - 128]], axis=1)
    grad_neighbor = jnp.concatenate([total[256:512], tail[:, 64 : CLS - 64]], axis=1)
    return (logits, tail[200, 127], grad_self, grad_neighbor, tail[:CLS, 127])


def solution(mesh):
    return jax.shard_map(
        shards,
        mesh=mesh,
        in_specs=(
            P("node", "feat", None),
            P("node", None, None),
            P("node", None),
            P("node", None, None, None),
            P("node", "feat"),
            P("node", "feat"),
            P(),
            P(),
            P(),
            P(),
            P(),
            P(),
        ),
        out_specs=(P("node", "feat", None), P(), P(), P(), P()),
        check_vma=False,
    )
```

```python
import functools
import math

import jax
import jax.numpy as jnp
from jax import lax
from jax.experimental import pallas as pl
from jax.experimental.pallas import tpu as pltpu
from jax.sharding import PartitionSpec as P

MESH = pl.DeviceIdType.MESH
F32 = jnp.float32
BF16 = jnp.bfloat16
NT_DIMS = (((1,), (1,)), ((), ()))
LANES = 128
SLOTS = 8
BLOCK = 8192
TILES = 64
GROUPS = 8
GROUP = 1024
CLS = 172
CLS_PAD = 176
PIECE = 24
HALF = 384


def iota(shape, axis):
    return lax.broadcasted_iota(jnp.int32, shape, axis)


def lanes(index, width=LANES):
    return pl.ds(pl.multiple_of(index * width, width), width)


def rows(index, height):
    return pl.ds(pl.multiple_of(index * height, height), height)


def loop(low, high, body):
    def step(i, carry):
        body(i)
        return carry

    lax.fori_loop(low, high, step, 0)


def permutation():
    j, p = iota((LANES, LANES), 0), iota((LANES, LANES), 1)
    return (j == 8 * (p % 16) + p // 16).astype(F32).astype(BF16)


def exchange_bits(words):
    group = iota(words.shape, 1) // 16
    for level, low_bits in ((0, 0x55555555), (1, 0x33333333), (2, 0x0F0F0F0F)):
        distance = 1 << level
        upper = ((group >> level) & 1) == 1
        keep = jnp.where(upper, ~jnp.int32(low_bits), jnp.int32(low_bits))
        from_above = pltpu.roll(words, LANES - 16 * distance, 1) << distance
        from_below = pltpu.roll(words, 16 * distance, 1) >> distance
        words = (words & keep) | (jnp.where(upper, from_below, from_above) & ~keep)
    return words


def unpack_row_tile(t, count_ref, bits, adj):
    limit = jnp.full((8, LANES), count_ref[0, t], jnp.int32)
    for pair in range(SLOTS // 2):
        packed = None
        for part in range(4):
            slot, half = 2 * pair + part // 2, part % 2
            piece = bits[t, pl.ds(64 * half + slot, 8, stride=8), :]
            piece = jnp.where(limit > slot, piece, 0) << (8 * part)
            packed = piece if packed is None else packed | piece
        packed = exchange_bits(packed)
        for side in range(2):
            slot = 2 * pair + side
            for low in range(8):
                first = (packed >> (16 * side + low)) & 1
                second = (packed >> (16 * side + 8 + low)) & 1
                both = jnp.concatenate([first, second], axis=0).astype(F32).astype(BF16)
                adj[t, 16 * low : 16 * low + 16, LANES * slot : LANES * (slot + 1)] = both


def picked_tiles(t, first_column, column_ref, table):
    parts = []
    for slot in range(SLOTS):
        index = jnp.clip(column_ref[slot, t] - first_column, 0, 3 * TILES - 1)
        parts.append(table[index])
    return jnp.concatenate(parts, axis=1)


def kernel(
    scale,
    features,
    bit_words,
    columns_in,
    count_in,
    labels_in,
    train_mask_in,
    first_self_in,
    first_neighbor_in,
    first_bias_in,
    second_self_in,
    second_neighbor_in,
    second_bias_in,
    logits_out,
    grad_self_out,
    grad_neighbor_out,
    grad_bias_out,
    loss_out,
    column_ref,
    count_ref,
    labels,
    train_mask,
    first_self,
    first_neighbor,
    first_bias,
    second_self,
    second_neighbor,
    second_bias,
    grad_self,
    grad_neighbor,
    grad_bias,
    loss_held,
    feats,
    bits,
    adj,
    table1,
    stage1,
    inputs1,
    table2,
    stage2,
    parts1,
    parts2,
    hidden,
    mean2,
    inv_degree,
    hidden_true,
    w1,
    w2,
    b1,
    b2,
    logits_rows,
    grad,
    payload,
    core_in,
    half_sum,
    plane_in,
    line_in,
    total,
    bit_sem,
    small_sem,
    local_sem,
    halo1_send,
    halo1_recv,
    x_send,
    x_recv,
    m_send,
    m_recv,
    h_send,
    h_recv,
    halo2_send,
    halo2_recv,
    n_send,
    n_recv,
    core_send,
    core_recv,
    plane_send,
    plane_recv,
    line_send,
    line_recv,
    back_send,
    back_recv,
):
    z = lax.axis_index("feat")
    node = lax.axis_index("node")
    core = lax.rem(node, 2)
    plane = lax.div(node, 2)
    up = lax.rem(node + 1, 32)
    down = lax.rem(node + 31, 32)
    core_peer = plane * 2 + 1 - core
    first_column = (node - 1) * TILES

    def around(offset):
        return lax.rem(z + offset, GROUPS)

    def plane_peer(offset):
        return lax.rem(plane + offset, 16)

    def send(src, dst, send_sem, recv_sem, device):
        return pltpu.make_async_remote_copy(
            src_ref=src,
            dst_ref=dst,
            send_sem=send_sem,
            recv_sem=recv_sem,
            device_id=device,
            device_id_type=MESH,
        )

    closing = []
    barrier = pltpu.get_barrier_semaphore()

    def greet(device):
        pl.semaphore_signal(barrier, inc=1, device_id=device, device_id_type=MESH)

    loop(1, GROUPS, lambda o: greet((around(o), node)))
    loop(1, 16, lambda o: greet((z, plane_peer(o) * 2 + core)))
    greet((z, up))
    greet((z, down))

    feature_copy = pltpu.make_async_copy(features.at[0], feats, local_sem.at[0])
    feature_copy.start()

    def bit_copy(r):
        return pltpu.make_async_copy(
            bit_words.at[0, :, :, lanes(r)], bits.at[:, rows(r, 8), :], bit_sem.at[r]
        )

    loop(0, 16, lambda r: bit_copy(r).start())
    small = [
        pltpu.make_async_copy(src, dst, small_sem.at[i])
        for i, (src, dst) in enumerate(
            (
                (columns_in, column_ref),
                (count_in, count_ref),
                (first_self_in, first_self),
                (first_neighbor_in, first_neighbor),
                (first_bias_in, first_bias),
                (second_self_in, second_self),
                (second_neighbor_in, second_neighbor),
                (second_bias_in, second_bias),
                (labels_in, labels),
                (train_mask_in, train_mask),
            )
        )
    ]
    for copy in small:
        copy.start()

    perm = permutation()
    feature_copy.wait()

    def permute_features(t):
        moved = jnp.dot(feats[:, lanes(t)], perm, preferred_element_type=F32)
        table1[TILES + t] = moved.astype(BF16)

    loop(0, TILES, permute_features)
    pl.semaphore_wait(barrier, 24)

    own1 = table1.at[pl.ds(TILES, TILES)]
    to_up1 = send(own1, table1.at[pl.ds(0, TILES)], halo1_send.at[0], halo1_recv.at[0], (z, up))
    to_down1 = send(own1, table1.at[pl.ds(2 * TILES, TILES)], halo1_send.at[1], halo1_recv.at[1], (z, down))
    to_up1.start()
    to_down1.start()
    closing.extend([to_up1.wait_send, to_down1.wait_send])

    def send_x(group, source):
        return send(
            table1.at[pl.ds(TILES + 8 * group, 8)],
            inputs1.at[source],
            x_send.at[group],
            x_recv.at[source],
            (group, node),
        )

    def send_m(group, source):
        return send(
            stage1.at[pl.ds(8 * group, 8)],
            inputs1.at[8 + source],
            m_send.at[group],
            m_recv.at[source],
            (group, node),
        )

    def send_h(group, source):
        return send(
            parts1.at[group],
            table2.at[pl.ds(TILES + 8 * source, 8)],
            h_send.at[group],
            h_recv.at[source],
            (group, node),
        )

    def send_n(group, source):
        return send(
            stage2.at[pl.ds(8 * group, 8)],
            parts2.at[source],
            n_send.at[group],
            n_recv.at[source],
            (group, node),
        )

    loop(1, GROUPS, lambda o: send_x(around(o), z).start())
    closing.append(lambda: loop(1, GROUPS, lambda o: send_x(around(o), z).wait_send()))
    x_own = pltpu.make_async_copy(
        table1.at[pl.ds(TILES + 8 * z, 8)], inputs1.at[z], local_sem.at[1]
    )
    x_own.start()

    for copy in small:
        copy.wait()

    eye = (iota((256, 256), 0) == iota((256, 256), 1)).astype(F32)
    for part, weight in enumerate((first_self, first_neighbor)):
        turned = lax.dot_general(eye.astype(BF16), weight[...], NT_DIMS, preferred_element_type=F32)
        w1[:, LANES * part : LANES * (part + 1)] = turned.astype(BF16)
    pick = (iota((CLS_PAD, CLS), 0) == iota((CLS_PAD, CLS), 1)).astype(F32)
    for part, weight in enumerate((second_self, second_neighbor)):
        padded = jnp.dot(pick.astype(BF16), weight[...], preferred_element_type=F32)
        w2[:, 256 * part : 256 * (part + 1)] = padded.astype(BF16)
    column1 = jnp.sum(jnp.where(eye > 0.5, first_bias[...], 0.0), axis=1, keepdims=True)
    b1[...] = jnp.broadcast_to(column1, (256, LANES))
    column2 = jnp.sum(jnp.where(pick > 0.5, second_bias[...], 0.0), axis=1, keepdims=True)
    column2 = jnp.where(iota((CLS_PAD, 1), 0) < CLS, column2, -1e30)
    b2[...] = jnp.broadcast_to(column2, (CLS_PAD, LANES))

    loop(0, 16, lambda r: bit_copy(r).wait())

    def unpack_some(i):
        for u in range(4):
            unpack_row_tile(i * 4 + u, count_ref, bits, adj)

    loop(0, TILES // 4, unpack_some)

    to_up1.wait_recv()
    to_down1.wait_recv()

    def first_tile(t):
        values = picked_tiles(t, first_column, column_ref, table1)
        stacked = jnp.concatenate([values, jnp.ones((16, SLOTS * LANES), BF16)], axis=0)
        sums = lax.dot_general(stacked, adj[t], NT_DIMS, preferred_element_type=F32)
        inverse = 1.0 / jnp.maximum(sums[16:24], 1.0)
        inv_degree[t] = inverse
        stage1[t] = (sums[:16] * inverse[:1]).astype(BF16)

    def first_group(o):
        group = around(o)
        for u in range(8):
            first_tile(group * 8 + u)

        @pl.when(o < GROUPS)
        def _():
            send_m(group, z).start()

    loop(1, GROUPS + 1, first_group)
    closing.append(lambda: loop(1, GROUPS, lambda o: send_m(around(o), z).wait_send()))
    m_own = pltpu.make_async_copy(
        stage1.at[pl.ds(8 * z, 8)], inputs1.at[8 + z], local_sem.at[2]
    )
    m_own.start()
    x_own.wait()
    m_own.wait()
    loop(1, GROUPS, lambda o: send_x(z, around(o)).wait_recv())
    loop(1, GROUPS, lambda o: send_m(z, around(o)).wait_recv())

    def first_dense(u):
        node_inputs = inputs1[:, u].reshape(256, LANES)
        total1 = jnp.dot(w1[...], node_inputs, preferred_element_type=F32)
        activated = jnp.maximum(total1 + b1[...], 0.0).astype(BF16)
        hidden[:, lanes(u)] = activated
        parts1[:, u] = activated.reshape(GROUPS, 32, LANES)

    loop(0, 8, first_dense)
    loop(1, GROUPS, lambda o: send_h(around(o), z).start())
    closing.append(lambda: loop(1, GROUPS, lambda o: send_h(around(o), z).wait_send()))
    table2[pl.ds(TILES + 8 * z, 8)] = parts1[z]

    def halo2(group, side, device):
        return send(
            table2.at[pl.ds(TILES + 8 * group, 8)],
            table2.at[pl.ds(2 * TILES * side + 8 * group, 8)],
            halo2_send.at[side, group],
            halo2_recv.at[side, group],
            (z, device),
        )

    def forward(group):
        halo2(group, 0, up).start()
        halo2(group, 1, down).start()

    forward(z)

    def restore(u):
        moved = lax.dot_general(hidden[:, lanes(u)], perm, NT_DIMS, preferred_element_type=F32)
        hidden_true[:, lanes(u)] = moved.astype(BF16)

    loop(0, 8, restore)

    def pass_on(o):
        group = around(o)
        send_h(z, group).wait_recv()
        forward(group)

    loop(1, GROUPS, pass_on)

    def halo2_left(group):
        halo2(group, 0, up).wait_send()
        halo2(group, 1, down).wait_send()

    closing.append(lambda: loop(0, GROUPS, halo2_left))
    def halo2_arrived(group):
        halo2(group, 0, up).wait_recv()
        halo2(group, 1, down).wait_recv()

    loop(0, GROUPS, halo2_arrived)

    def second_tile(t):
        values = picked_tiles(t, first_column, column_ref, table2)
        sums = lax.dot_general(values, adj[t], NT_DIMS, preferred_element_type=F32)
        stage2[t] = (sums * inv_degree[t][:1]).astype(BF16)

    def second_group(o):
        group = around(o)
        for u in range(8):
            second_tile(group * 8 + u)

        @pl.when(o < GROUPS)
        def _():
            send_n(group, z).start()

    loop(1, GROUPS + 1, second_group)
    closing.append(lambda: loop(1, GROUPS, lambda o: send_n(around(o), z).wait_send()))
    parts2[z] = stage2[pl.ds(8 * z, 8)]
    loop(1, GROUPS, lambda o: send_n(z, around(o)).wait_recv())

    def second_dense(u, loss):
        span = lanes(u)
        moved = lax.dot_general(
            parts2[:, u].reshape(256, LANES), perm, NT_DIMS, preferred_element_type=F32
        )
        mean2[:, span] = moved.astype(BF16)
        score = (
            jnp.dot(w2[:, :256], hidden_true[:, span], preferred_element_type=F32)
            + jnp.dot(w2[:, 256:], mean2[:, span], preferred_element_type=F32)
            + b2[...]
        )
        logits_rows[:, :, span] = score[:CLS].reshape(CLS, 1, LANES)
        exponent = jnp.exp(score)
        class_total = jnp.sum(exponent, axis=0, keepdims=True)
        weight = train_mask[:, span].astype(F32)
        chosen = iota((CLS_PAD, LANES), 0) == labels[:, span]
        own_score = jnp.sum(jnp.where(chosen, score, 0.0), axis=0, keepdims=True)
        slope = exponent * (1.0 / class_total) - jnp.where(chosen, 1.0, 0.0)
        grad[0:CLS_PAD, span] = (slope * (weight * scale)).astype(BF16)
        return loss + (jnp.log(class_total) - own_score) * weight

    grad[CLS_PAD:256, :] = jnp.zeros((256 - CLS_PAD, GROUP), BF16)
    loss_lanes = lax.fori_loop(0, 8, second_dense, jnp.zeros((1, LANES), F32))
    logits_copy = pltpu.make_async_copy(logits_rows, logits_out, local_sem.at[3])
    logits_copy.start()
    closing.append(logits_copy.wait)
    for part, values in enumerate((hidden_true, mean2)):
        product = lax.dot_general(grad[0:CLS_PAD], values[...], NT_DIMS, preferred_element_type=F32)
        payload[2 * part * CLS_PAD : (2 * part + 1) * CLS_PAD] = product[:, :LANES]
        payload[(2 * part + 1) * CLS_PAD : (2 * part + 2) * CLS_PAD] = product[:, LANES:]
    bias = lax.dot_general(
        jnp.ones((16, GROUP), BF16), grad[...], NT_DIMS, preferred_element_type=F32
    )
    payload[704:712] = bias[:8, :LANES]
    payload[712:720] = bias[:8, LANES:]
    loss = jnp.sum(loss_lanes, axis=1, keepdims=True) * (scale * scale)
    payload[720:728] = jnp.broadcast_to(loss, (8, LANES))
    payload[728:768] = jnp.zeros((40, LANES), F32)

    core_copy = send(
        payload.at[rows(1 - core, HALF), :], core_in, core_send.at[0], core_recv.at[0], (z, core_peer)
    )
    core_copy.start()
    closing.append(core_copy.wait_send)
    core_copy.wait_recv()
    half_sum[...] = payload[rows(core, HALF), :] + core_in[...]

    def plane_copy(target, source):
        return send(
            half_sum.at[rows(target, PIECE), :],
            plane_in.at[source],
            plane_send.at[target],
            plane_recv.at[source],
            (z, target * 2 + core),
        )

    loop(1, 16, lambda o: plane_copy(plane_peer(o), plane).start())
    closing.append(lambda: loop(1, 16, lambda o: plane_copy(plane_peer(o), plane).wait_send()))
    plane_in[plane] = half_sum[rows(plane, PIECE), :]
    loop(1, 16, lambda o: plane_copy(plane, plane_peer(o)).wait_recv())
    line_in[z] = jnp.sum(plane_in[...], axis=0)

    def line_copy(target, source):
        return send(
            line_in.at[source], line_in.at[source], line_send.at[target], line_recv.at[source], (target, node)
        )

    loop(1, GROUPS, lambda o: line_copy(around(o), z).start())
    closing.append(lambda: loop(1, GROUPS, lambda o: line_copy(around(o), z).wait_send()))
    loop(1, GROUPS, lambda o: line_copy(z, around(o)).wait_recv())
    total[rows(core * 16 + plane, PIECE), :] = jnp.sum(line_in[...], axis=0)

    def back_copy(target, source):
        part = total.at[rows(core * 16 + source, PIECE), :]
        return send(part, part, back_send.at[target], back_recv.at[source], (z, target * 2 + core))

    loop(1, 16, lambda o: back_copy(plane_peer(o), plane).start())
    closing.append(lambda: loop(1, 16, lambda o: back_copy(plane_peer(o), plane).wait_send()))
    loop(1, 16, lambda o: back_copy(plane, plane_peer(o)).wait_recv())

    def half_copy(which):
        part = total.at[rows(which, HALF), :]
        return send(part, part, core_send.at[1], core_recv.at[1], (z, core_peer))

    half_copy(core).start()
    closing.append(half_copy(core).wait_send)
    half_copy(1 - core).wait_recv()
    for part, held in enumerate((grad_self, grad_neighbor)):
        for side in range(2):
            start = (2 * part + side) * CLS_PAD
            held[:, LANES * side : LANES * (side + 1)] = total[start : start + CLS]
    grad_bias[:, :LANES] = total[704:705]
    grad_bias[:, LANES:] = total[712:713, : CLS - LANES]
    loss_held[...] = total[720:721, :1]
    results = (
        (grad_self, grad_self_out),
        (grad_neighbor, grad_neighbor_out),
        (grad_bias, grad_bias_out),
        (loss_held, loss_out),
    )
    for i, (src, dst) in enumerate(results):
        copy = pltpu.make_async_copy(src, dst, small_sem.at[i])
        copy.start()
        closing.append(copy.wait)

    for wait in closing:
        wait()


def hand_over(*refs):
    sources, targets, places, arrive, leave = refs[:5], refs[5:10], refs[10:15], refs[15], refs[16]
    inward = [
        pltpu.make_async_copy(src, place, arrive.at[i])
        for i, (src, place) in enumerate(zip(sources, places))
    ]
    outward = [
        pltpu.make_async_copy(place, dst, leave.at[i])
        for i, (place, dst) in enumerate(zip(places, targets))
    ]
    for copy in inward:
        copy.start()
    for first, second in zip(inward, outward):
        first.wait()
        second.start()
    for copy in outward:
        copy.wait()


def shards(
    features,
    tile_columns,
    tile_count,
    tile_bits,
    labels,
    train_mask,
    first_self,
    first_neighbor,
    first_bias,
    second_self,
    second_neighbor,
    second_bias,
):
    node_total = features.shape[2] * lax.axis_size("node")
    dma = pltpu.SemaphoreType.DMA
    anywhere = pl.BlockSpec(memory_space=pl.ANY)
    results = (
        jax.ShapeDtypeStruct((CLS, 1, GROUP), F32),
        jax.ShapeDtypeStruct((CLS, 256), F32),
        jax.ShapeDtypeStruct((CLS, 256), F32),
        jax.ShapeDtypeStruct((1, CLS), F32),
        jax.ShapeDtypeStruct((1, 1), F32),
    )
    held = pl.pallas_call(
        functools.partial(kernel, 1.0 / math.sqrt(node_total)),
        out_shape=results,
        in_specs=[anywhere] * 12,
        out_specs=(anywhere,) * 5,
        scratch_shapes=[
            pltpu.SMEM((SLOTS, TILES), jnp.int32),
            pltpu.SMEM((1, TILES), jnp.int32),
            pltpu.VMEM((1, GROUP), jnp.int32),
            pltpu.VMEM((1, GROUP), jnp.int32),
            pltpu.VMEM((LANES, 256), BF16),
            pltpu.VMEM((LANES, 256), BF16),
            pltpu.VMEM((1, 256), F32),
            pltpu.VMEM((CLS, 256), BF16),
            pltpu.VMEM((CLS, 256), BF16),
            pltpu.VMEM((1, CLS), F32),
            pltpu.VMEM((CLS, 256), F32),
            pltpu.VMEM((CLS, 256), F32),
            pltpu.VMEM((1, CLS), F32),
            pltpu.VMEM((1, 1), F32),
            pltpu.VMEM((16, BLOCK), BF16),
            pltpu.VMEM((TILES, 128, LANES), jnp.int32),
            pltpu.VMEM((TILES, LANES, SLOTS * LANES), BF16),
            pltpu.VMEM((3 * TILES, 16, LANES), BF16),
            pltpu.VMEM((TILES, 16, LANES), BF16),
            pltpu.VMEM((2 * GROUPS, 8, 16, LANES), BF16),
            pltpu.VMEM((3 * TILES, 32, LANES), BF16),
            pltpu.VMEM((TILES, 32, LANES), BF16),
            pltpu.VMEM((GROUPS, 8, 32, LANES), BF16),
            pltpu.VMEM((GROUPS, 8, 32, LANES), BF16),
            pltpu.VMEM((256, GROUP), BF16),
            pltpu.VMEM((256, GROUP), BF16),
            pltpu.VMEM((TILES, 8, LANES), F32),
            pltpu.VMEM((256, GROUP), BF16),
            pltpu.VMEM((256, 256), BF16),
            pltpu.VMEM((CLS_PAD, 512), BF16),
            pltpu.VMEM((256, LANES), F32),
            pltpu.VMEM((CLS_PAD, LANES), F32),
            pltpu.VMEM((CLS, 1, GROUP), F32),
            pltpu.VMEM((256, GROUP), BF16),
            pltpu.VMEM((2 * HALF, LANES), F32),
            pltpu.VMEM((HALF, LANES), F32),
            pltpu.VMEM((HALF, LANES), F32),
            pltpu.VMEM((16, PIECE, LANES), F32),
            pltpu.VMEM((GROUPS, PIECE, LANES), F32),
            pltpu.VMEM((2 * HALF, LANES), F32),
            dma((16,)),
            dma((10,)),
            dma((4,)),
            dma((2,)),
            dma((2,)),
            dma((GROUPS,)),
            dma((GROUPS,)),
            dma((GROUPS,)),
            dma((GROUPS,)),
            dma((GROUPS,)),
            dma((GROUPS,)),
            dma((2, GROUPS)),
            dma((2, GROUPS)),
            dma((GROUPS,)),
            dma((GROUPS,)),
            dma((2,)),
            dma((2,)),
            dma((16,)),
            dma((16,)),
            dma((GROUPS,)),
            dma((GROUPS,)),
            dma((16,)),
            dma((16,)),
        ],
        compiler_params=pltpu.CompilerParams(
            collective_id=0, has_side_effects=True, vmem_limit_bytes=62 * 1024 * 1024
        ),
    )(
        features,
        tile_bits,
        tile_columns[0].T,
        tile_count,
        labels,
        train_mask,
        first_self,
        first_neighbor,
        first_bias[None],
        second_self.T,
        second_neighbor.T,
        second_bias[None],
    )
    logits, grad_self, grad_neighbor, grad_bias, loss = pl.pallas_call(
        hand_over,
        out_shape=results,
        in_specs=[anywhere] * 5,
        out_specs=(anywhere,) * 5,
        scratch_shapes=[pltpu.VMEM(r.shape, F32) for r in results] + [dma((5,)), dma((5,))],
        compiler_params=pltpu.CompilerParams(vmem_limit_bytes=62 * 1024 * 1024),
    )(*held)
    logits = jnp.transpose(logits, (1, 2, 0))
    return (logits, loss[0, 0], grad_self.T, grad_neighbor.T, grad_bias[0])


def solution(mesh):
    return jax.shard_map(
        shards,
        mesh=mesh,
        in_specs=(
            P("node", "feat", None),
            P("node", None, None),
            P("node", None),
            P("node", None, None, None),
            P("node", "feat"),
            P("node", "feat"),
            P(),
            P(),
            P(),
            P(),
            P(),
            P(),
        ),
        out_specs=(P("node", "feat", None), P(), P(), P(), P()),
        check_vma=False,
    )
```

```python
import functools
import math

import jax
import jax.numpy as jnp
from jax import lax
from jax.experimental import pallas as pl
from jax.experimental.pallas import tpu as pltpu
from jax.sharding import PartitionSpec as P

MESH = pl.DeviceIdType.MESH
F32 = jnp.float32
BF16 = jnp.bfloat16
NT_DIMS = (((1,), (1,)), ((), ()))
LANES = 128
SLOTS = 8
BLOCK = 8192
TILES = 64
GROUPS = 8
GROUP = 1024
CLS = 172
CLS_PAD = 176
PIECE = 24
HALF = 384


def iota(shape, axis):
    return lax.broadcasted_iota(jnp.int32, shape, axis)


def lanes(index, width=LANES):
    return pl.ds(pl.multiple_of(index * width, width), width)


def rows(index, height):
    return pl.ds(pl.multiple_of(index * height, height), height)


def loop(low, high, body):
    def step(i, carry):
        body(i)
        return carry

    lax.fori_loop(low, high, step, 0)


def permutation():
    j, p = iota((LANES, LANES), 0), iota((LANES, LANES), 1)
    return (j == 8 * (p % 16) + p // 16).astype(F32).astype(BF16)


def exchange_bits(words):
    group = iota(words.shape, 1) // 16
    for level, low_bits in ((0, 0x55555555), (1, 0x33333333), (2, 0x0F0F0F0F)):
        distance = 1 << level
        upper = ((group >> level) & 1) == 1
        keep = jnp.where(upper, ~jnp.int32(low_bits), jnp.int32(low_bits))
        from_above = pltpu.roll(words, LANES - 16 * distance, 1) << distance
        from_below = pltpu.roll(words, 16 * distance, 1) >> distance
        words = (words & keep) | (jnp.where(upper, from_below, from_above) & ~keep)
    return words


def unpack_row_tile(t, count_ref, bits, adj):
    limit = jnp.full((8, LANES), count_ref[0, t], jnp.int32)
    for pair in range(SLOTS // 2):
        packed = None
        for part in range(4):
            slot, half = 2 * pair + part // 2, part % 2
            piece = bits[t, pl.ds(64 * half + slot, 8, stride=8), :]
            piece = jnp.where(limit > slot, piece, 0) << (8 * part)
            packed = piece if packed is None else packed | piece
        packed = exchange_bits(packed)
        for side in range(2):
            slot = 2 * pair + side
            for low in range(8):
                first = (packed >> (16 * side + low)) & 1
                second = (packed >> (16 * side + 8 + low)) & 1
                both = jnp.concatenate([first, second], axis=0).astype(F32).astype(BF16)
                adj[t, 16 * low : 16 * low + 16, LANES * slot : LANES * (slot + 1)] = both


def picked_tiles(t, first_column, column_ref, table):
    parts = []
    for slot in range(SLOTS):
        index = jnp.clip(column_ref[slot, t] - first_column, 0, 3 * TILES - 1)
        parts.append(table[index])
    return jnp.concatenate(parts, axis=1)


def kernel(
    scale,
    features,
    bit_words,
    columns_in,
    count_in,
    labels_in,
    train_mask_in,
    first_self_in,
    first_neighbor_in,
    first_bias_in,
    second_self_in,
    second_neighbor_in,
    second_bias_in,
    logits_out,
    grad_self_out,
    grad_neighbor_out,
    grad_bias_out,
    loss_out,
    column_ref,
    count_ref,
    labels,
    train_mask,
    first_self,
    first_neighbor,
    first_bias,
    second_self,
    second_neighbor,
    second_bias,
    grad_self,
    grad_neighbor,
    grad_bias,
    loss_held,
    feats,
    bits,
    adj,
    table1,
    stage1,
    inputs1,
    table2,
    stage2,
    parts1,
    parts2,
    hidden,
    inv_degree,
    second_inputs,
    own_scores,
    w1,
    w2,
    b1,
    b2,
    logits_rows,
    grad,
    payload,
    core_in,
    half_sum,
    plane_in,
    line_in,
    total,
    bit_sem,
    small_sem,
    local_sem,
    halo1_send,
    halo1_recv,
    x_send,
    x_recv,
    m_send,
    m_recv,
    h_send,
    h_recv,
    halo2_send,
    halo2_recv,
    n_send,
    n_recv,
    core_send,
    core_recv,
    plane_send,
    plane_recv,
    line_send,
    line_recv,
    back_send,
    back_recv,
):
    z = lax.axis_index("feat")
    node = lax.axis_index("node")
    core = lax.rem(node, 2)
    plane = lax.div(node, 2)
    up = lax.rem(node + 1, 32)
    down = lax.rem(node + 31, 32)
    core_peer = plane * 2 + 1 - core
    first_column = (node - 1) * TILES

    def around(offset):
        return lax.rem(z + offset, GROUPS)

    def far_first(i):
        return around(4 + lax.div(i + 1, 2) * (1 - 2 * lax.rem(i, 2)))

    plane_x, plane_y = lax.div(plane, 4), lax.rem(plane, 4)
    plane_peers = [
        lax.rem(plane_x + dx, 4) * 4 + lax.rem(plane_y + dy, 4)
        for dx in (2, 1, 3, 0)
        for dy in (2, 1, 3, 0)
        if dx or dy
    ]

    def send(src, dst, send_sem, recv_sem, device):
        return pltpu.make_async_remote_copy(
            src_ref=src,
            dst_ref=dst,
            send_sem=send_sem,
            recv_sem=recv_sem,
            device_id=device,
            device_id_type=MESH,
        )

    closing = []
    barrier = pltpu.get_barrier_semaphore()

    def greet(device):
        pl.semaphore_signal(barrier, inc=1, device_id=device, device_id_type=MESH)

    loop(1, GROUPS, lambda o: greet((around(o), node)))
    for peer in plane_peers:
        greet((z, peer * 2 + core))
    greet((z, up))
    greet((z, down))

    feature_copy = pltpu.make_async_copy(features.at[0], feats, local_sem.at[0])
    feature_copy.start()

    def bit_copy(r):
        return pltpu.make_async_copy(
            bit_words.at[0, :, :, lanes(r)], bits.at[:, rows(r, 8), :], bit_sem.at[r]
        )

    loop(0, 16, lambda r: bit_copy(r).start())
    small = [
        pltpu.make_async_copy(src, dst, small_sem.at[i])
        for i, (src, dst) in enumerate(
            (
                (columns_in, column_ref),
                (count_in, count_ref),
                (first_self_in, first_self),
                (first_neighbor_in, first_neighbor),
                (first_bias_in, first_bias),
                (second_self_in, second_self),
                (second_neighbor_in, second_neighbor),
                (second_bias_in, second_bias),
                (labels_in, labels),
                (train_mask_in, train_mask),
            )
        )
    ]
    for copy in small:
        copy.start()

    perm = permutation()
    feature_copy.wait()

    def permute_features(i):
        for u in range(16):
            moved = jnp.dot(feats[:, lanes(16 * i + u)], perm, preferred_element_type=F32)
            table1[TILES + 16 * i + u] = moved.astype(BF16)

    loop(0, TILES // 16, permute_features)
    pl.semaphore_wait(barrier, 24)

    own1 = table1.at[pl.ds(TILES, TILES)]
    to_up1 = send(own1, table1.at[pl.ds(0, TILES)], halo1_send.at[0], halo1_recv.at[0], (z, up))
    to_down1 = send(own1, table1.at[pl.ds(2 * TILES, TILES)], halo1_send.at[1], halo1_recv.at[1], (z, down))
    to_up1.start()
    to_down1.start()
    closing.extend([to_up1.wait_send, to_down1.wait_send])

    def send_x(group, source):
        return send(
            table1.at[pl.ds(TILES + 8 * group, 8)],
            inputs1.at[source],
            x_send.at[group],
            x_recv.at[source],
            (group, node),
        )

    def send_m(group, source, half):
        return send(
            stage1.at[pl.ds(8 * group + 4 * half, 4)],
            inputs1.at[8 + source, pl.ds(4 * half, 4)],
            m_send.at[half, group],
            m_recv.at[half, source],
            (group, node),
        )

    def send_h(group, source, half):
        return send(
            parts1.at[group, pl.ds(4 * half, 4)],
            table2.at[pl.ds(TILES + 8 * source + 4 * half, 4)],
            h_send.at[half, group],
            h_recv.at[half, source],
            (group, node),
        )

    def send_n(group, source, half):
        return send(
            stage2.at[pl.ds(8 * group + 4 * half, 4)],
            parts2.at[source, pl.ds(4 * half, 4)],
            n_send.at[half, group],
            n_recv.at[half, source],
            (group, node),
        )

    others = range(GROUPS - 1)
    for i in others:
        send_x(far_first(i), z).start()
    closing.append(lambda: loop(1, GROUPS, lambda o: send_x(around(o), z).wait_send()))
    inputs1[z] = table1[pl.ds(TILES + 8 * z, 8)]

    for copy in small:
        copy.wait()

    eye = (iota((256, 256), 0) == iota((256, 256), 1)).astype(F32)
    for part, weight in enumerate((first_self, first_neighbor)):
        turned = lax.dot_general(eye.astype(BF16), weight[...], NT_DIMS, preferred_element_type=F32)
        w1[:, LANES * part : LANES * (part + 1)] = turned.astype(BF16)
    pick = (iota((CLS_PAD, CLS), 0) == iota((CLS_PAD, CLS), 1)).astype(F32)
    for part, weight in enumerate((second_self, second_neighbor)):
        padded = jnp.dot(pick.astype(BF16), weight[...], preferred_element_type=F32)
        w2[:, 256 * part : 256 * (part + 1)] = padded.astype(BF16)
    column1 = jnp.sum(jnp.where(eye > 0.5, first_bias[...], 0.0), axis=1, keepdims=True)
    b1[...] = jnp.broadcast_to(column1, (256, LANES))
    column2 = jnp.sum(jnp.where(pick > 0.5, second_bias[...], 0.0), axis=1, keepdims=True)
    column2 = jnp.where(iota((CLS_PAD, 1), 0) < CLS, column2, -1e30)
    b2[...] = jnp.broadcast_to(column2, (CLS_PAD, LANES))

    loop(0, 16, lambda r: bit_copy(r).wait())

    def unpack_some(i):
        for u in range(4):
            unpack_row_tile(i * 4 + u, count_ref, bits, adj)

    loop(0, TILES // 4, unpack_some)

    to_up1.wait_recv()
    to_down1.wait_recv()

    def first_tile(t):
        values = picked_tiles(t, first_column, column_ref, table1)
        stacked = jnp.concatenate([values, jnp.ones((16, SLOTS * LANES), BF16)], axis=0)
        sums = lax.dot_general(stacked, adj[t], NT_DIMS, preferred_element_type=F32)
        inverse = 1.0 / jnp.maximum(sums[16:24], 1.0)
        inv_degree[t] = inverse
        stage1[t] = (sums[:16] * inverse[:1]).astype(BF16)

    def aggregate(tile, send_part, half):
        def two_groups(i):
            pair = [far_first(2 * i), far_first(2 * i + 1)]
            for group in pair:
                for u in range(4):
                    tile(group * 8 + 4 * half + u)
            send_part(pair[0], z, half).start()

            @pl.when(i < 3)
            def _():
                send_part(pair[1], z, half).start()

        loop(0, 4, two_groups)

    def all_left(send_part):
        def left(o):
            for half in range(2):
                send_part(around(o), z, half).wait_send()

        closing.append(lambda: loop(1, GROUPS, left))

    def all_arrived(send_part, half):
        loop(1, GROUPS, lambda o: send_part(z, around(o), half).wait_recv())

    for half in range(2):
        aggregate(first_tile, send_m, half)
    all_left(send_m)

    def halo2(group, half, side, device):
        return send(
            table2.at[pl.ds(TILES + 8 * group + 4 * half, 4)],
            table2.at[pl.ds(2 * TILES * side + 8 * group + 4 * half, 4)],
            halo2_send.at[side, half, group],
            halo2_recv.at[side, half, group],
            (z, device),
        )

    def forward(group, half):
        halo2(group, half, 0, up).start()
        halo2(group, half, 1, down).start()

    loop(1, GROUPS, lambda o: send_x(z, around(o)).wait_recv())
    for half in range(2):
        tiles = pl.ds(4 * half, 4)
        inputs1[8 + z, tiles] = stage1[pl.ds(8 * z + 4 * half, 4)]
        all_arrived(send_m, half)
        for u in range(4 * half, 4 * half + 4):
            node_inputs = inputs1[:, u].reshape(256, LANES)
            total1 = jnp.dot(w1[...], node_inputs, preferred_element_type=F32)
            activated = jnp.maximum(total1 + b1[...], 0.0).astype(BF16)
            hidden[:, LANES * u : LANES * (u + 1)] = activated
            parts1[:, u] = activated.reshape(GROUPS, 32, LANES)
        for i in others:
            send_h(far_first(i), z, half).start()
        table2[pl.ds(TILES + 8 * z + 4 * half, 4)] = parts1[z, tiles]
        forward(z, half)
    all_left(send_h)

    for u in range(8):
        span = slice(LANES * u, LANES * (u + 1))
        moved = lax.dot_general(hidden[:, span], perm, NT_DIMS, preferred_element_type=F32)
        moved = moved.astype(BF16)
        second_inputs[0, :, span] = moved
        own_part = jnp.dot(w2[:, :256], moved, preferred_element_type=F32)
        own_scores[:, span] = own_part + b2[...]

    for half in range(2):

        def pass_on(i):
            group = far_first(i)
            send_h(z, group, half).wait_recv()
            forward(group, half)

        loop(0, GROUPS - 1, pass_on)

    def halo2_left(group):
        for half in range(2):
            halo2(group, half, 0, up).wait_send()
            halo2(group, half, 1, down).wait_send()

    closing.append(lambda: loop(0, GROUPS, halo2_left))

    def halo2_arrived(group):
        for half in range(2):
            halo2(group, half, 0, up).wait_recv()
            halo2(group, half, 1, down).wait_recv()

    loop(0, GROUPS, halo2_arrived)

    def second_tile(t):
        values = picked_tiles(t, first_column, column_ref, table2)
        sums = lax.dot_general(values, adj[t], NT_DIMS, preferred_element_type=F32)
        stage2[t] = (sums * inv_degree[t][:1]).astype(BF16)

    for half in range(2):
        aggregate(second_tile, send_n, half)
    all_left(send_n)

    grad[CLS_PAD:256, :] = jnp.zeros((256 - CLS_PAD, GROUP), BF16)
    loss_lanes = jnp.zeros((1, LANES), F32)

    def gradient(part, half):
        span = slice(512 * half, 512 * (half + 1))
        product = lax.dot_general(
            grad[0:CLS_PAD, span],
            second_inputs[part, :, span],
            NT_DIMS,
            preferred_element_type=F32,
        )
        for side in range(2):
            place = pl.ds(pl.multiple_of(HALF * part + CLS_PAD * side, 8), CLS_PAD)
            values = product[:, LANES * side : LANES * (side + 1)]
            payload[place] = values if half == 0 else payload[place] + values

    for half in range(2):
        parts2[z, pl.ds(4 * half, 4)] = stage2[pl.ds(8 * z + 4 * half, 4)]
        all_arrived(send_n, half)
        for u in range(4 * half, 4 * half + 4):
            span = slice(LANES * u, LANES * (u + 1))
            moved = lax.dot_general(
                parts2[:, u].reshape(256, LANES), perm, NT_DIMS, preferred_element_type=F32
            )
            moved = moved.astype(BF16)
            second_inputs[1, :, span] = moved
            score = own_scores[:, span] + jnp.dot(w2[:, 256:], moved, preferred_element_type=F32)
            logits_rows[:, :, span] = score[:CLS].reshape(CLS, 1, LANES)
            exponent = jnp.exp(score)
            class_total = jnp.sum(exponent, axis=0, keepdims=True)
            weight = train_mask[:, span].astype(F32)
            chosen = iota((CLS_PAD, LANES), 0) == labels[:, span]
            own_score = jnp.sum(jnp.where(chosen, score, 0.0), axis=0, keepdims=True)
            slope = exponent * (1.0 / class_total) - jnp.where(chosen, 1.0, 0.0)
            grad[0:CLS_PAD, span] = (slope * (weight * scale)).astype(BF16)
            loss_lanes = loss_lanes + (jnp.log(class_total) - own_score) * weight
        if half == 0:
            gradient(0, 0)
            gradient(1, 0)

    bias = lax.dot_general(
        jnp.ones((16, GROUP), BF16), grad[...], NT_DIMS, preferred_element_type=F32
    )
    loss = jnp.sum(loss_lanes, axis=1, keepdims=True) * (scale * scale)
    for part in range(2):
        start = HALF * part + 2 * CLS_PAD
        payload[start : start + 8] = bias[:8, :LANES]
        payload[start + 8 : start + 16] = bias[:8, LANES:]
        payload[start + 16 : start + 24] = jnp.broadcast_to(loss, (8, LANES))
        payload[start + 24 : start + 32] = jnp.zeros((8, LANES), F32)
    gradient(1 - core, 1)

    core_copy = send(
        payload.at[rows(1 - core, HALF), :], core_in, core_send.at[0], core_recv.at[0], (z, core_peer)
    )
    core_copy.start()
    closing.append(core_copy.wait_send)
    gradient(core, 1)
    logits_copy = pltpu.make_async_copy(logits_rows, logits_out, local_sem.at[3])
    logits_copy.start()
    closing.append(logits_copy.wait)
    core_copy.wait_recv()
    half_sum[...] = payload[rows(core, HALF), :] + core_in[...]

    def plane_copy(target, source):
        return send(
            half_sum.at[rows(target, PIECE), :],
            plane_in.at[source],
            plane_send.at[target],
            plane_recv.at[source],
            (z, target * 2 + core),
        )

    for peer in plane_peers:
        plane_copy(peer, plane).start()
        closing.append(plane_copy(peer, plane).wait_send)
    plane_in[plane] = half_sum[rows(plane, PIECE), :]
    for peer in plane_peers:
        plane_copy(plane, peer).wait_recv()
    line_in[z] = jnp.sum(plane_in[...], axis=0)

    def line_copy(target, source):
        return send(
            line_in.at[source], line_in.at[source], line_send.at[target], line_recv.at[source], (target, node)
        )

    for i in others:
        line_copy(far_first(i), z).start()
    closing.append(lambda: loop(1, GROUPS, lambda o: line_copy(around(o), z).wait_send()))
    loop(1, GROUPS, lambda o: line_copy(z, around(o)).wait_recv())
    total[rows(core * 16 + plane, PIECE), :] = jnp.sum(line_in[...], axis=0)

    def back_copy(target, source):
        part = total.at[rows(core * 16 + source, PIECE), :]
        return send(part, part, back_send.at[target], back_recv.at[source], (z, target * 2 + core))

    for peer in plane_peers:
        back_copy(peer, plane).start()
        closing.append(back_copy(peer, plane).wait_send)
    for peer in plane_peers:
        back_copy(plane, peer).wait_recv()

    def half_copy(which):
        part = total.at[rows(which, HALF), :]
        return send(part, part, core_send.at[1], core_recv.at[1], (z, core_peer))

    half_copy(core).start()
    closing.append(half_copy(core).wait_send)
    half_copy(1 - core).wait_recv()
    for part, held in enumerate((grad_self, grad_neighbor)):
        for side in range(2):
            start = HALF * part + CLS_PAD * side
            held[:, LANES * side : LANES * (side + 1)] = total[start : start + CLS]
    grad_bias[:, :LANES] = total[352:353]
    grad_bias[:, LANES:] = total[360:361, : CLS - LANES]
    loss_held[...] = total[368:369, :1]
    results = (
        (grad_self, grad_self_out),
        (grad_neighbor, grad_neighbor_out),
        (grad_bias, grad_bias_out),
        (loss_held, loss_out),
    )
    for i, (src, dst) in enumerate(results):
        copy = pltpu.make_async_copy(src, dst, small_sem.at[i])
        copy.start()
        closing.append(copy.wait)

    for wait in closing:
        wait()


def hand_over(*refs):
    sources, targets, places, arrive, leave = refs[:5], refs[5:10], refs[10:15], refs[15], refs[16]
    inward = [
        pltpu.make_async_copy(src, place, arrive.at[i])
        for i, (src, place) in enumerate(zip(sources, places))
    ]
    outward = [
        pltpu.make_async_copy(place, dst, leave.at[i])
        for i, (place, dst) in enumerate(zip(places, targets))
    ]
    for copy in inward:
        copy.start()
    for first, second in zip(inward, outward):
        first.wait()
        second.start()
    for copy in outward:
        copy.wait()


def shards(
    features,
    tile_columns,
    tile_count,
    tile_bits,
    labels,
    train_mask,
    first_self,
    first_neighbor,
    first_bias,
    second_self,
    second_neighbor,
    second_bias,
):
    node_total = features.shape[2] * lax.axis_size("node")
    dma = pltpu.SemaphoreType.DMA
    anywhere = pl.BlockSpec(memory_space=pl.ANY)
    results = (
        jax.ShapeDtypeStruct((CLS, 1, GROUP), F32),
        jax.ShapeDtypeStruct((CLS, 256), F32),
        jax.ShapeDtypeStruct((CLS, 256), F32),
        jax.ShapeDtypeStruct((1, CLS), F32),
        jax.ShapeDtypeStruct((1, 1), F32),
    )
    held = pl.pallas_call(
        functools.partial(kernel, 1.0 / math.sqrt(node_total)),
        out_shape=results,
        in_specs=[anywhere] * 12,
        out_specs=(anywhere,) * 5,
        scratch_shapes=[
            pltpu.SMEM((SLOTS, TILES), jnp.int32),
            pltpu.SMEM((1, TILES), jnp.int32),
            pltpu.VMEM((1, GROUP), jnp.int32),
            pltpu.VMEM((1, GROUP), jnp.int32),
            pltpu.VMEM((LANES, 256), BF16),
            pltpu.VMEM((LANES, 256), BF16),
            pltpu.VMEM((1, 256), F32),
            pltpu.VMEM((CLS, 256), BF16),
            pltpu.VMEM((CLS, 256), BF16),
            pltpu.VMEM((1, CLS), F32),
            pltpu.VMEM((CLS, 256), F32),
            pltpu.VMEM((CLS, 256), F32),
            pltpu.VMEM((1, CLS), F32),
            pltpu.VMEM((1, 1), F32),
            pltpu.VMEM((16, BLOCK), BF16),
            pltpu.VMEM((TILES, 128, LANES), jnp.int32),
            pltpu.VMEM((TILES, LANES, SLOTS * LANES), BF16),
            pltpu.VMEM((3 * TILES, 16, LANES), BF16),
            pltpu.VMEM((TILES, 16, LANES), BF16),
            pltpu.VMEM((2 * GROUPS, 8, 16, LANES), BF16),
            pltpu.VMEM((3 * TILES, 32, LANES), BF16),
            pltpu.VMEM((TILES, 32, LANES), BF16),
            pltpu.VMEM((GROUPS, 8, 32, LANES), BF16),
            pltpu.VMEM((GROUPS, 8, 32, LANES), BF16),
            pltpu.VMEM((256, GROUP), BF16),
            pltpu.VMEM((TILES, 8, LANES), F32),
            pltpu.VMEM((2, 256, GROUP), BF16),
            pltpu.VMEM((CLS_PAD, GROUP), F32),
            pltpu.VMEM((256, 256), BF16),
            pltpu.VMEM((CLS_PAD, 512), BF16),
            pltpu.VMEM((256, LANES), F32),
            pltpu.VMEM((CLS_PAD, LANES), F32),
            pltpu.VMEM((CLS, 1, GROUP), F32),
            pltpu.VMEM((256, GROUP), BF16),
            pltpu.VMEM((2 * HALF, LANES), F32),
            pltpu.VMEM((HALF, LANES), F32),
            pltpu.VMEM((HALF, LANES), F32),
            pltpu.VMEM((16, PIECE, LANES), F32),
            pltpu.VMEM((GROUPS, PIECE, LANES), F32),
            pltpu.VMEM((2 * HALF, LANES), F32),
            dma((16,)),
            dma((10,)),
            dma((4,)),
            dma((2,)),
            dma((2,)),
            dma((GROUPS,)),
            dma((GROUPS,)),
            dma((2, GROUPS)),
            dma((2, GROUPS)),
            dma((2, GROUPS)),
            dma((2, GROUPS)),
            dma((2, 2, GROUPS)),
            dma((2, 2, GROUPS)),
            dma((2, GROUPS)),
            dma((2, GROUPS)),
            dma((2,)),
            dma((2,)),
            dma((16,)),
            dma((16,)),
            dma((GROUPS,)),
            dma((GROUPS,)),
            dma((16,)),
            dma((16,)),
        ],
        compiler_params=pltpu.CompilerParams(
            collective_id=0, has_side_effects=True, vmem_limit_bytes=62 * 1024 * 1024
        ),
    )(
        features,
        tile_bits,
        tile_columns[0].T,
        tile_count,
        labels,
        train_mask,
        first_self,
        first_neighbor,
        first_bias[None],
        second_self.T,
        second_neighbor.T,
        second_bias[None],
    )
    logits, grad_self, grad_neighbor, grad_bias, loss = pl.pallas_call(
        hand_over,
        out_shape=results,
        in_specs=[anywhere] * 5,
        out_specs=(anywhere,) * 5,
        scratch_shapes=[pltpu.VMEM(r.shape, F32) for r in results] + [dma((5,)), dma((5,))],
        compiler_params=pltpu.CompilerParams(vmem_limit_bytes=62 * 1024 * 1024),
    )(*held)
    logits = jnp.transpose(logits, (1, 2, 0))
    return (logits, loss[0, 0], grad_self.T, grad_neighbor.T, grad_bias[0])


def solution(mesh):
    return jax.shard_map(
        shards,
        mesh=mesh,
        in_specs=(
            P("node", "feat", None),
            P("node", None, None),
            P("node", None),
            P("node", None, None, None),
            P("node", "feat"),
            P("node", "feat"),
            P(),
            P(),
            P(),
            P(),
            P(),
            P(),
        ),
        out_specs=(P("node", "feat", None), P(), P(), P(), P()),
        check_vma=False,
    )
```

```python
import functools
import math

import jax
import jax.numpy as jnp
from jax import lax
from jax.experimental import pallas as pl
from jax.experimental.pallas import tpu as pltpu
from jax.sharding import PartitionSpec as P

MESH = pl.DeviceIdType.MESH
F32 = jnp.float32
BF16 = jnp.bfloat16
NT_DIMS = (((1,), (1,)), ((), ()))
LANES = 128
SLOTS = 8
BLOCK = 8192
TILES = 64
GROUPS = 8
GROUP = 1024
CLS = 172
CLS_PAD = 176
PIECE = 24
FIRST_PARTS = 2
SECOND_PARTS = 2
HALF = 384


def iota(shape, axis):
    return lax.broadcasted_iota(jnp.int32, shape, axis)


def lanes(index, width=LANES):
    return pl.ds(pl.multiple_of(index * width, width), width)


def rows(index, height):
    return pl.ds(pl.multiple_of(index * height, height), height)


def loop(low, high, body):
    def step(i, carry):
        body(i)
        return carry

    lax.fori_loop(low, high, step, 0)


def permutation():
    j, p = iota((LANES, LANES), 0), iota((LANES, LANES), 1)
    return (j == 8 * (p % 16) + p // 16).astype(F32).astype(BF16)


def exchange_bits(words):
    group = iota(words.shape, 1) // 16
    for level, low_bits in ((0, 0x55555555), (1, 0x33333333), (2, 0x0F0F0F0F)):
        distance = 1 << level
        upper = ((group >> level) & 1) == 1
        keep = jnp.where(upper, ~jnp.int32(low_bits), jnp.int32(low_bits))
        from_above = pltpu.roll(words, LANES - 16 * distance, 1) << distance
        from_below = pltpu.roll(words, 16 * distance, 1) >> distance
        words = (words & keep) | (jnp.where(upper, from_below, from_above) & ~keep)
    return words


def unpack_row_tile(t, count_ref, bits, adj):
    limit = jnp.full((8, LANES), count_ref[0, t], jnp.int32)
    for pair in range(SLOTS // 2):
        packed = None
        for part in range(4):
            slot, half = 2 * pair + part // 2, part % 2
            piece = bits[t, pl.ds(64 * half + slot, 8, stride=8), :]
            piece = jnp.where(limit > slot, piece, 0) << (8 * part)
            packed = piece if packed is None else packed | piece
        packed = exchange_bits(packed)
        for side in range(2):
            slot = 2 * pair + side
            part = packed >> 16 if side else packed
            for low in range(8):
                first = part & (1 << low)
                second = part & (256 << low)
                both = jnp.concatenate([first, second], axis=0).astype(F32).astype(BF16)
                adj[t, 16 * low : 16 * low + 16, LANES * slot : LANES * (slot + 1)] = both


def picked_tiles(t, first_column, column_ref, table):
    parts = []
    for slot in range(SLOTS):
        index = jnp.clip(column_ref[slot, t] - first_column, 0, 3 * TILES - 1)
        parts.append(table[index])
    return jnp.concatenate(parts, axis=1)


def kernel(
    scale,
    features,
    bit_words,
    columns_in,
    count_in,
    labels_in,
    train_mask_in,
    first_self_in,
    first_neighbor_in,
    first_bias_in,
    second_self_in,
    second_neighbor_in,
    second_bias_in,
    logits_out,
    grad_self_out,
    grad_neighbor_out,
    grad_bias_out,
    loss_out,
    column_ref,
    count_ref,
    labels,
    train_mask,
    first_self,
    first_neighbor,
    first_bias,
    second_self,
    second_neighbor,
    second_bias,
    grad_self,
    grad_neighbor,
    grad_bias,
    loss_held,
    feats,
    bits,
    adj,
    table1,
    stage1,
    inputs1,
    table2,
    stage2,
    parts1,
    parts2,
    hidden,
    inv_degree,
    second_inputs,
    own_scores,
    w1,
    w2,
    b1,
    b2,
    logits_rows,
    grad,
    payload,
    core_in,
    half_sum,
    plane_in,
    line_in,
    total,
    bit_sem,
    small_sem,
    local_sem,
    halo1_send,
    halo1_recv,
    x_send,
    x_recv,
    m_send,
    m_recv,
    h_send,
    h_recv,
    halo2_send,
    halo2_recv,
    n_send,
    n_recv,
    core_send,
    core_recv,
    plane_send,
    plane_recv,
    line_send,
    line_recv,
    back_send,
    back_recv,
):
    z = lax.axis_index("feat")
    node = lax.axis_index("node")
    core = lax.rem(node, 2)
    plane = lax.div(node, 2)
    up = lax.rem(node + 1, 32)
    down = lax.rem(node + 31, 32)
    core_peer = plane * 2 + 1 - core
    first_column = (node - 1) * TILES

    def around(offset):
        return lax.rem(z + offset, GROUPS)

    def far_first(i):
        return around(4 + lax.div(i + 1, 2) * (1 - 2 * lax.rem(i, 2)))

    plane_x, plane_y = lax.div(plane, 4), lax.rem(plane, 4)
    plane_peers = [
        lax.rem(plane_x + dx, 4) * 4 + lax.rem(plane_y + dy, 4)
        for dx in (2, 1, 3, 0)
        for dy in (2, 1, 3, 0)
        if dx or dy
    ]

    def send(src, dst, send_sem, recv_sem, device):
        return pltpu.make_async_remote_copy(
            src_ref=src,
            dst_ref=dst,
            send_sem=send_sem,
            recv_sem=recv_sem,
            device_id=device,
            device_id_type=MESH,
        )

    def drain(ref, sem):
        send(ref, ref, sem, sem, (z, up)).wait_recv()

    closing = []

    def close():
        while closing:
            closing.pop(0)()

    barrier = pltpu.get_barrier_semaphore()

    def greet(device):
        pl.semaphore_signal(barrier, inc=1, device_id=device, device_id_type=MESH)

    loop(1, GROUPS, lambda o: greet((around(o), node)))
    for peer in plane_peers:
        greet((z, peer * 2 + core))
    greet((z, up))
    greet((z, down))

    feature_copy = pltpu.make_async_copy(features.at[0], feats, local_sem.at[0])
    feature_copy.start()

    def bit_copy(r):
        return pltpu.make_async_copy(
            bit_words.at[0, :, :, lanes(r)], bits.at[:, rows(r, 8), :], bit_sem.at[r]
        )

    loop(0, 16, lambda r: bit_copy(r).start())
    small = [
        pltpu.make_async_copy(src, dst, small_sem.at[i])
        for i, (src, dst) in enumerate(
            (
                (columns_in, column_ref),
                (count_in, count_ref),
                (first_self_in, first_self),
                (first_neighbor_in, first_neighbor),
                (first_bias_in, first_bias),
                (second_self_in, second_self),
                (second_neighbor_in, second_neighbor),
                (second_bias_in, second_bias),
                (labels_in, labels),
                (train_mask_in, train_mask),
            )
        )
    ]
    for copy in small:
        copy.start()

    perm = permutation()
    feature_copy.wait()

    def permute_features(i):
        for u in range(16):
            moved = jnp.dot(feats[:, lanes(16 * i + u)], perm, preferred_element_type=F32)
            table1[TILES + 16 * i + u] = moved.astype(BF16)

    loop(0, TILES // 16, permute_features)
    pl.semaphore_wait(barrier, 24)

    own1 = table1.at[pl.ds(TILES, TILES)]
    to_up1 = send(own1, table1.at[pl.ds(0, TILES)], halo1_send.at[0], halo1_recv.at[0], (z, up))
    to_down1 = send(own1, table1.at[pl.ds(2 * TILES, TILES)], halo1_send.at[1], halo1_recv.at[1], (z, down))
    to_up1.start()
    to_down1.start()
    closing.extend([to_up1.wait_send, to_down1.wait_send])
    size1, size2 = 8 // FIRST_PARTS, 8 // SECOND_PARTS

    def send_x(group, source):
        return send(
            table1.at[pl.ds(TILES + 8 * group, 8)],
            inputs1.at[source],
            x_send,
            x_recv,
            (group, node),
        )

    def send_m(group, source, part):
        return send(
            stage1.at[pl.ds(8 * group + size1 * part, size1)],
            inputs1.at[8 + source, pl.ds(size1 * part, size1)],
            m_send,
            m_recv.at[part],
            (group, node),
        )

    def send_h(group, source, part):
        return send(
            parts1.at[group, pl.ds(size1 * part, size1)],
            table2.at[pl.ds(TILES + 8 * source + size1 * part, size1)],
            h_send,
            h_recv.at[part, source],
            (group, node),
        )

    def send_n(group, source, part):
        return send(
            stage2.at[pl.ds(8 * group + size2 * part, size2)],
            parts2.at[source, pl.ds(size2 * part, size2)],
            n_send,
            n_recv.at[part],
            (group, node),
        )

    others = range(GROUPS - 1)
    for i in others:
        send_x(far_first(i), z).start()
    closing.append(lambda: drain(inputs1.at[0:7], x_send))
    inputs1[z] = table1[pl.ds(TILES + 8 * z, 8)]

    for copy in small[:2]:
        copy.wait()

    loop(0, 16, lambda r: bit_copy(r).wait())

    def unpack_some(i):
        for u in range(4):
            unpack_row_tile(i * 4 + u, count_ref, bits, adj)

    loop(0, TILES // 4, unpack_some)

    to_up1.wait_recv()
    to_down1.wait_recv()

    place = iota((8, LANES), 1)
    exponents = place // 16 + 8 * ((place // 8) % 2)
    unscale = jnp.ones((8, LANES), F32)
    for bit in range(4):
        unscale = unscale * jnp.where((exponents >> bit) & 1 == 1, 0.5 ** (1 << bit), 1.0)

    def first_tile(t):
        values = picked_tiles(t, first_column, column_ref, table1)
        stacked = jnp.concatenate([values, jnp.ones((16, SLOTS * LANES), BF16)], axis=0)
        sums = lax.dot_general(stacked, adj[t], NT_DIMS, preferred_element_type=F32)
        inverse = unscale / jnp.maximum(sums[16:24] * unscale, 1.0)
        inv_degree[t] = inverse
        stage1[t] = (sums[:16] * inverse[:1]).astype(BF16)

    def aggregate(tile, send_part, part, size):
        count = 8 // size

        def some_groups(i):
            groups = [far_first(count * i + k) for k in range(count)]
            for group in groups:
                for u in range(size):
                    tile(group * 8 + size * part + u)
            for group in groups[:-1]:
                send_part(group, z, part).start()

            @pl.when(i < size - 1)
            def _():
                send_part(groups[-1], z, part).start()

        loop(0, size, some_groups)

    for part in range(FIRST_PARTS):
        aggregate(first_tile, send_m, part, size1)
    closing.append(lambda: drain(inputs1.at[8:15], m_send))

    def halo2(group, part, side, device):
        return send(
            table2.at[pl.ds(TILES + 8 * group + size1 * part, size1)],
            table2.at[pl.ds(2 * TILES * side + 8 * group + size1 * part, size1)],
            halo2_send.at[side],
            halo2_recv.at[side],
            (z, device),
        )

    def forward(group, part):
        halo2(group, part, 0, up).start()
        halo2(group, part, 1, down).start()

    for copy in small[2:]:
        copy.wait()

    eye = (iota((256, 256), 0) == iota((256, 256), 1)).astype(F32)
    for part, weight in enumerate((first_self, first_neighbor)):
        turned = lax.dot_general(eye.astype(BF16), weight[...], NT_DIMS, preferred_element_type=F32)
        w1[:, LANES * part : LANES * (part + 1)] = turned.astype(BF16)
    pick = (iota((CLS_PAD, CLS), 0) == iota((CLS_PAD, CLS), 1)).astype(F32)
    for part, weight in enumerate((second_self, second_neighbor)):
        padded = jnp.dot(pick.astype(BF16), weight[...], preferred_element_type=F32)
        w2[:, 256 * part : 256 * (part + 1)] = padded.astype(BF16)
    column1 = jnp.sum(jnp.where(eye > 0.5, first_bias[...], 0.0), axis=1, keepdims=True)
    b1[...] = jnp.broadcast_to(column1, (256, LANES))
    column2 = jnp.sum(jnp.where(pick > 0.5, second_bias[...], 0.0), axis=1, keepdims=True)
    column2 = jnp.where(iota((CLS_PAD, 1), 0) < CLS, column2, -1e30)
    b2[...] = jnp.broadcast_to(column2, (CLS_PAD, LANES))

    drain(inputs1.at[0:7], x_recv)
    for part in range(FIRST_PARTS):
        tiles = pl.ds(size1 * part, size1)
        inputs1[8 + z, tiles] = stage1[pl.ds(8 * z + size1 * part, size1)]
        drain(inputs1.at[8:15, tiles], m_recv.at[part])
        for u in range(size1 * part, size1 * (part + 1)):
            node_inputs = inputs1[:, u].reshape(256, LANES)
            total1 = jnp.dot(w1[...], node_inputs, preferred_element_type=F32)
            activated = jnp.maximum(total1 + b1[...], 0.0).astype(BF16)
            hidden[:, LANES * u : LANES * (u + 1)] = activated
            parts1[:, u] = activated.reshape(GROUPS, 32, LANES)
        for i in others:
            send_h(far_first(i), z, part).start()
        table2[pl.ds(TILES + 8 * z + size1 * part, size1)] = parts1[z, tiles]
        forward(z, part)
    closing.append(lambda: drain(parts1.at[0:7], h_send))

    for u in range(8):
        span = slice(LANES * u, LANES * (u + 1))
        moved = lax.dot_general(hidden[:, span], perm, NT_DIMS, preferred_element_type=F32)
        moved = moved.astype(BF16)
        second_inputs[0, :, span] = moved
        own_part = jnp.dot(w2[:, :256], moved, preferred_element_type=F32)
        own_scores[:, span] = own_part + b2[...]

    for part in range(FIRST_PARTS):

        def pass_on(i):
            group = far_first(i)
            send_h(z, group, part).wait_recv()
            forward(group, part)

        loop(0, GROUPS - 1, pass_on)

    for side in range(2):
        block = table2.at[pl.ds(2 * TILES * side, TILES)]
        closing.append(functools.partial(drain, block, halo2_send.at[side]))
        drain(block, halo2_recv.at[side])

    def second_tile(t):
        values = picked_tiles(t, first_column, column_ref, table2)
        sums = lax.dot_general(values, adj[t], NT_DIMS, preferred_element_type=F32)
        stage2[t] = (sums * inv_degree[t][:1]).astype(BF16)

    for part in range(SECOND_PARTS):
        aggregate(second_tile, send_n, part, size2)
    closing.append(lambda: drain(parts2.at[0:7], n_send))

    grad[CLS_PAD:256, :] = jnp.zeros((256 - CLS_PAD, GROUP), BF16)
    loss_lanes = jnp.zeros((1, LANES), F32)

    def gradient(part, half):
        span = slice(512 * half, 512 * (half + 1))
        product = lax.dot_general(
            grad[0:CLS_PAD, span],
            second_inputs[part, :, span],
            NT_DIMS,
            preferred_element_type=F32,
        )
        for side in range(2):
            place = pl.ds(pl.multiple_of(HALF * part + CLS_PAD * side, 8), CLS_PAD)
            values = product[:, LANES * side : LANES * (side + 1)]
            payload[place] = values if half == 0 else payload[place] + values

    for half in range(2):
        parts2[z, pl.ds(4 * half, 4)] = stage2[pl.ds(8 * z + 4 * half, 4)]
        drain(parts2.at[0:7, pl.ds(4 * half, 4)], n_recv.at[half])
        for u in range(4 * half, 4 * half + 4):
            span = slice(LANES * u, LANES * (u + 1))
            moved = lax.dot_general(
                parts2[:, u].reshape(256, LANES), perm, NT_DIMS, preferred_element_type=F32
            )
            moved = moved.astype(BF16)
            second_inputs[1, :, span] = moved
            score = own_scores[:, span] + jnp.dot(w2[:, 256:], moved, preferred_element_type=F32)
            logits_rows[:, :, span] = score[:CLS].reshape(CLS, 1, LANES)
            exponent = jnp.exp(score)
            class_total = jnp.sum(exponent, axis=0, keepdims=True)
            weight = train_mask[:, span].astype(F32)
            chosen = iota((CLS_PAD, LANES), 0) == labels[:, span]
            own_score = jnp.sum(jnp.where(chosen, score, 0.0), axis=0, keepdims=True)
            slope = exponent * (1.0 / class_total) - jnp.where(chosen, 1.0, 0.0)
            grad[0:CLS_PAD, span] = (slope * (weight * scale)).astype(BF16)
            loss_lanes = loss_lanes + (jnp.log(class_total) - own_score) * weight
        if half == 0:
            gradient(0, 0)
            gradient(1, 0)

    bias = lax.dot_general(
        jnp.ones((16, GROUP), BF16), grad[...], NT_DIMS, preferred_element_type=F32
    )
    loss = jnp.sum(loss_lanes, axis=1, keepdims=True) * (scale * scale)
    for part in range(2):
        start = HALF * part + 2 * CLS_PAD
        payload[start : start + 8] = bias[:8, :LANES]
        payload[start + 8 : start + 16] = bias[:8, LANES:]
        payload[start + 16 : start + 24] = jnp.broadcast_to(loss, (8, LANES))
        payload[start + 24 : start + 32] = jnp.zeros((8, LANES), F32)
    gradient(1 - core, 1)

    core_copy = send(
        payload.at[rows(1 - core, HALF), :], core_in, core_send.at[0], core_recv.at[0], (z, core_peer)
    )
    core_copy.start()
    closing.append(core_copy.wait_send)
    gradient(core, 1)
    logits_copy = pltpu.make_async_copy(logits_rows, logits_out, local_sem.at[3])
    logits_copy.start()
    closing.append(logits_copy.wait)
    core_copy.wait_recv()
    half_sum[...] = payload[rows(core, HALF), :] + core_in[...]

    def plane_copy(target, source):
        return send(
            half_sum.at[rows(target, PIECE), :],
            plane_in.at[source],
            plane_send,
            plane_recv,
            (z, target * 2 + core),
        )

    for peer in plane_peers:
        plane_copy(peer, plane).start()
    close()
    closing.append(lambda: drain(plane_in.at[0:15], plane_send))
    plane_in[plane] = half_sum[rows(plane, PIECE), :]
    drain(plane_in.at[0:15], plane_recv)
    line_in[z] = jnp.sum(plane_in[...], axis=0)

    def line_copy(target, source):
        return send(
            line_in.at[source], line_in.at[source], line_send, line_recv, (target, node)
        )

    for i in others:
        line_copy(far_first(i), z).start()
    close()
    closing.append(lambda: drain(line_in.at[0:7], line_send))
    drain(line_in.at[0:7], line_recv)
    total[rows(core * 16 + plane, PIECE), :] = jnp.sum(line_in[...], axis=0)

    def back_copy(target, source):
        part = total.at[rows(core * 16 + source, PIECE), :]
        return send(part, part, back_send, back_recv, (z, target * 2 + core))

    for peer in plane_peers:
        back_copy(peer, plane).start()
    close()
    pieces = total.at[0 : 15 * PIECE]
    drain(pieces, back_recv)
    closing.append(lambda: drain(pieces, back_send))

    def half_copy(which):
        part = total.at[rows(which, HALF), :]
        return send(part, part, core_send.at[1], core_recv.at[1], (z, core_peer))

    half_copy(core).start()
    closing.append(half_copy(core).wait_send)
    half_copy(1 - core).wait_recv()
    for part, held in enumerate((grad_self, grad_neighbor)):
        for side in range(2):
            start = HALF * part + CLS_PAD * side
            held[:, LANES * side : LANES * (side + 1)] = total[start : start + CLS]
    grad_bias[:, :LANES] = total[352:353]
    grad_bias[:, LANES:] = total[360:361, : CLS - LANES]
    loss_held[...] = total[368:369, :1]
    results = (
        (grad_self, grad_self_out),
        (grad_neighbor, grad_neighbor_out),
        (grad_bias, grad_bias_out),
        (loss_held, loss_out),
    )
    for i, (src, dst) in enumerate(results):
        copy = pltpu.make_async_copy(src, dst, small_sem.at[i])
        copy.start()
        closing.append(copy.wait)

    close()


def hand_over(*refs):
    sources, targets, places, arrive, leave = refs[:5], refs[5:10], refs[10:15], refs[15], refs[16]
    quarter = CLS // 4
    cuts = [(k, slice(None)) for k in range(1, 5)]
    cuts += [(0, slice(k * quarter, (k + 1) * quarter)) for k in range(4)]
    inward, outward = [], []
    for i, (k, cut) in enumerate(cuts):
        place = places[k].at[cut]
        inward.append(pltpu.make_async_copy(sources[k].at[cut], place, arrive.at[i]))
        outward.append(pltpu.make_async_copy(place, targets[k].at[cut], leave.at[i]))
    for copy in inward:
        copy.start()
    for first, second in zip(inward, outward):
        first.wait()
        second.start()
    for copy in outward:
        copy.wait()


def shards(
    features,
    tile_columns,
    tile_count,
    tile_bits,
    labels,
    train_mask,
    first_self,
    first_neighbor,
    first_bias,
    second_self,
    second_neighbor,
    second_bias,
):
    node_total = features.shape[2] * lax.axis_size("node")
    dma = pltpu.SemaphoreType.DMA
    anywhere = pl.BlockSpec(memory_space=pl.ANY)
    results = (
        jax.ShapeDtypeStruct((CLS, 1, GROUP), F32),
        jax.ShapeDtypeStruct((CLS, 256), F32),
        jax.ShapeDtypeStruct((CLS, 256), F32),
        jax.ShapeDtypeStruct((1, CLS), F32),
        jax.ShapeDtypeStruct((1, 1), F32),
    )
    held = pl.pallas_call(
        functools.partial(kernel, 1.0 / math.sqrt(node_total)),
        out_shape=results,
        in_specs=[anywhere] * 12,
        out_specs=(anywhere,) * 5,
        scratch_shapes=[
            pltpu.SMEM((SLOTS, TILES), jnp.int32),
            pltpu.SMEM((1, TILES), jnp.int32),
            pltpu.VMEM((1, GROUP), jnp.int32),
            pltpu.VMEM((1, GROUP), jnp.int32),
            pltpu.VMEM((LANES, 256), BF16),
            pltpu.VMEM((LANES, 256), BF16),
            pltpu.VMEM((1, 256), F32),
            pltpu.VMEM((CLS, 256), BF16),
            pltpu.VMEM((CLS, 256), BF16),
            pltpu.VMEM((1, CLS), F32),
            pltpu.VMEM((CLS, 256), F32),
            pltpu.VMEM((CLS, 256), F32),
            pltpu.VMEM((1, CLS), F32),
            pltpu.VMEM((1, 1), F32),
            pltpu.VMEM((16, BLOCK), BF16),
            pltpu.VMEM((TILES, 128, LANES), jnp.int32),
            pltpu.VMEM((TILES, LANES, SLOTS * LANES), BF16),
            pltpu.VMEM((3 * TILES, 16, LANES), BF16),
            pltpu.VMEM((TILES, 16, LANES), BF16),
            pltpu.VMEM((2 * GROUPS, 8, 16, LANES), BF16),
            pltpu.VMEM((3 * TILES, 32, LANES), BF16),
            pltpu.VMEM((TILES, 32, LANES), BF16),
            pltpu.VMEM((GROUPS, 8, 32, LANES), BF16),
            pltpu.VMEM((GROUPS, 8, 32, LANES), BF16),
            pltpu.VMEM((256, GROUP), BF16),
            pltpu.VMEM((TILES, 8, LANES), F32),
            pltpu.VMEM((2, 256, GROUP), BF16),
            pltpu.VMEM((CLS_PAD, GROUP), F32),
            pltpu.VMEM((256, 256), BF16),
            pltpu.VMEM((CLS_PAD, 512), BF16),
            pltpu.VMEM((256, LANES), F32),
            pltpu.VMEM((CLS_PAD, LANES), F32),
            pltpu.VMEM((CLS, 1, GROUP), F32),
            pltpu.VMEM((256, GROUP), BF16),
            pltpu.VMEM((2 * HALF, LANES), F32),
            pltpu.VMEM((HALF, LANES), F32),
            pltpu.VMEM((HALF, LANES), F32),
            pltpu.VMEM((16, PIECE, LANES), F32),
            pltpu.VMEM((GROUPS, PIECE, LANES), F32),
            pltpu.VMEM((2 * HALF, LANES), F32),
            dma((16,)),
            dma((10,)),
            dma((4,)),
            dma((2,)),
            dma((2,)),
            dma(()),
            dma(()),
            dma(()),
            dma((FIRST_PARTS,)),
            dma(()),
            dma((FIRST_PARTS, GROUPS)),
            dma((2,)),
            dma((2,)),
            dma(()),
            dma((SECOND_PARTS,)),
            dma((2,)),
            dma((2,)),
            dma(()),
            dma(()),
            dma(()),
            dma(()),
            dma(()),
            dma(()),
        ],
        compiler_params=pltpu.CompilerParams(
            collective_id=0, has_side_effects=True, vmem_limit_bytes=62 * 1024 * 1024
        ),
    )(
        features,
        tile_bits,
        tile_columns[0].T,
        tile_count,
        labels,
        train_mask,
        first_self,
        first_neighbor,
        first_bias[None],
        second_self.T,
        second_neighbor.T,
        second_bias[None],
    )
    logits, grad_self, grad_neighbor, grad_bias, loss = pl.pallas_call(
        hand_over,
        out_shape=results,
        in_specs=[anywhere] * 5,
        out_specs=(anywhere,) * 5,
        scratch_shapes=[pltpu.VMEM(r.shape, F32) for r in results] + [dma((8,)), dma((8,))],
        compiler_params=pltpu.CompilerParams(vmem_limit_bytes=62 * 1024 * 1024),
    )(*held)
    logits = jnp.transpose(logits, (1, 2, 0))
    return (logits, loss[0, 0], grad_self.T, grad_neighbor.T, grad_bias[0])


def solution(mesh):
    return jax.shard_map(
        shards,
        mesh=mesh,
        in_specs=(
            P("node", "feat", None),
            P("node", None, None),
            P("node", None),
            P("node", None, None, None),
            P("node", "feat"),
            P("node", "feat"),
            P(),
            P(),
            P(),
            P(),
            P(),
            P(),
        ),
        out_specs=(P("node", "feat", None), P(), P(), P(), P()),
        check_vma=False,
    )
```

```python
import functools
import math

import jax
import jax.numpy as jnp
from jax import lax
from jax.experimental import pallas as pl
from jax.experimental.pallas import tpu as pltpu
from jax.sharding import PartitionSpec as P

MESH = pl.DeviceIdType.MESH
F32 = jnp.float32
BF16 = jnp.bfloat16
NT_DIMS = (((1,), (1,)), ((), ()))
LANES = 128
SLOTS = 8
BLOCK = 8192
TILES = 64
GROUPS = 8
GROUP = 1024
CLS = 172
CLS_PAD = 176
PIECE = 24
FIRST_PARTS = 2
SECOND_PARTS = 2
HALF = 384


def iota(shape, axis):
    return lax.broadcasted_iota(jnp.int32, shape, axis)


def lanes(index, width=LANES):
    return pl.ds(pl.multiple_of(index * width, width), width)


def rows(index, height):
    return pl.ds(pl.multiple_of(index * height, height), height)


def loop(low, high, body):
    def step(i, carry):
        body(i)
        return carry

    lax.fori_loop(low, high, step, 0)


def permutation():
    j, p = iota((LANES, LANES), 0), iota((LANES, LANES), 1)
    return (j == 8 * (p % 16) + p // 16).astype(F32).astype(BF16)


def exchange_bits(words):
    group = iota(words.shape, 1) // 16
    for level, low_bits in ((0, 0x55555555), (1, 0x33333333), (2, 0x0F0F0F0F)):
        distance = 1 << level
        upper = ((group >> level) & 1) == 1
        keep = jnp.where(upper, ~jnp.int32(low_bits), jnp.int32(low_bits))
        from_above = pltpu.roll(words, LANES - 16 * distance, 1) << distance
        from_below = pltpu.roll(words, 16 * distance, 1) >> distance
        words = (words & keep) | (jnp.where(upper, from_below, from_above) & ~keep)
    return words


def unpack_row_tile(t, count_ref, bits, adj):
    limit = jnp.full((8, LANES), count_ref[0, t], jnp.int32)
    for pair in range(SLOTS // 2):
        packed = None
        for part in range(4):
            slot, half = 2 * pair + part // 2, part % 2
            piece = bits[t, pl.ds(64 * half + slot, 8, stride=8), :]
            piece = jnp.where(limit > slot, piece, 0) << (8 * part)
            packed = piece if packed is None else packed | piece
        packed = exchange_bits(packed)
        for side in range(2):
            slot = 2 * pair + side
            part = packed >> 16 if side else packed
            for low in range(8):
                first = part & (1 << low)
                second = part & (256 << low)
                both = jnp.concatenate([first, second], axis=0).astype(F32).astype(BF16)
                adj[t, 16 * low : 16 * low + 16, LANES * slot : LANES * (slot + 1)] = both


def picked_tiles(t, first_column, column_ref, table):
    parts = []
    for slot in range(SLOTS):
        index = jnp.clip(column_ref[slot, t] - first_column, 0, 3 * TILES - 1)
        parts.append(table[index])
    return jnp.concatenate(parts, axis=1)


def kernel(
    scale,
    features,
    bit_words,
    columns_in,
    count_in,
    labels_in,
    train_mask_in,
    first_self_in,
    first_neighbor_in,
    first_bias_in,
    second_self_in,
    second_neighbor_in,
    second_bias_in,
    logits_out,
    grad_self_out,
    grad_neighbor_out,
    grad_bias_out,
    loss_out,
    column_ref,
    count_ref,
    labels,
    train_mask,
    first_self,
    first_neighbor,
    first_bias,
    second_self,
    second_neighbor,
    second_bias,
    grad_self,
    grad_neighbor,
    grad_bias,
    loss_held,
    feats,
    bits,
    adj,
    table1,
    stage1,
    inputs1,
    table2,
    stage2,
    parts1,
    parts2,
    hidden,
    inv_degree,
    second_inputs,
    own_scores,
    w1,
    w2,
    b1,
    b2,
    logits_rows,
    grad,
    payload,
    core_in,
    half_sum,
    plane_in,
    line_in,
    total,
    bit_sem,
    small_sem,
    local_sem,
    halo1_send,
    halo1_recv,
    x_send,
    x_recv,
    m_send,
    m_recv,
    h_send,
    h_recv,
    halo2_send,
    halo2_recv,
    n_send,
    n_recv,
    core_send,
    core_recv,
    plane_send,
    plane_recv,
    line_send,
    line_recv,
    back_send,
    back_recv,
):
    z = lax.axis_index("feat")
    node = lax.axis_index("node")
    core = lax.rem(node, 2)
    plane = lax.div(node, 2)
    up = lax.rem(node + 1, 32)
    down = lax.rem(node + 31, 32)
    core_peer = plane * 2 + 1 - core
    first_column = (node - 1) * TILES

    def around(offset):
        return lax.rem(z + offset, GROUPS)

    def far_first(i):
        return around(4 + lax.div(i + 1, 2) * (1 - 2 * lax.rem(i, 2)))

    plane_x, plane_y = lax.div(plane, 4), lax.rem(plane, 4)
    plane_peers = [
        lax.rem(plane_x + dx, 4) * 4 + lax.rem(plane_y + dy, 4)
        for dx in (2, 1, 3, 0)
        for dy in (2, 1, 3, 0)
        if dx or dy
    ]

    def send(src, dst, send_sem, recv_sem, device):
        return pltpu.make_async_remote_copy(
            src_ref=src,
            dst_ref=dst,
            send_sem=send_sem,
            recv_sem=recv_sem,
            device_id=device,
            device_id_type=MESH,
        )

    def drain(ref, sem):
        send(ref, ref, sem, sem, (z, up)).wait_recv()

    closing = []

    def close():
        while closing:
            closing.pop(0)()

    barrier = pltpu.get_barrier_semaphore()

    def greet(device):
        pl.semaphore_signal(barrier, inc=1, device_id=device, device_id_type=MESH)

    loop(1, GROUPS, lambda o: greet((around(o), node)))
    for peer in plane_peers:
        greet((z, peer * 2 + core))
    greet((z, up))
    greet((z, down))

    feature_copy = pltpu.make_async_copy(features.at[0], feats, local_sem.at[0])
    feature_copy.start()

    def bit_copy(r):
        return pltpu.make_async_copy(
            bit_words.at[0, :, :, lanes(r)], bits.at[:, rows(r, 8), :], bit_sem.at[r]
        )

    loop(0, 16, lambda r: bit_copy(r).start())
    small = [
        pltpu.make_async_copy(src, dst, small_sem.at[i])
        for i, (src, dst) in enumerate(
            (
                (columns_in, column_ref),
                (count_in, count_ref),
                (first_self_in, first_self),
                (first_neighbor_in, first_neighbor),
                (first_bias_in, first_bias),
                (second_self_in, second_self),
                (second_neighbor_in, second_neighbor),
                (second_bias_in, second_bias),
                (labels_in, labels),
                (train_mask_in, train_mask),
            )
        )
    ]
    for copy in small:
        copy.start()

    perm = permutation()
    feature_copy.wait()

    def permute_features(i):
        for u in range(16):
            moved = jnp.dot(feats[:, lanes(16 * i + u)], perm, preferred_element_type=F32)
            table1[TILES + 16 * i + u] = moved.astype(BF16)

    loop(0, TILES // 16, permute_features)
    pl.semaphore_wait(barrier, 24)

    own1 = table1.at[pl.ds(TILES, TILES)]
    to_up1 = send(own1, table1.at[pl.ds(0, TILES)], halo1_send.at[0], halo1_recv.at[0], (z, up))
    to_down1 = send(own1, table1.at[pl.ds(2 * TILES, TILES)], halo1_send.at[1], halo1_recv.at[1], (z, down))
    to_up1.start()
    to_down1.start()
    closing.extend([to_up1.wait_send, to_down1.wait_send])
    size1, size2 = 8 // FIRST_PARTS, 8 // SECOND_PARTS

    def send_x(group, source):
        return send(
            table1.at[pl.ds(TILES + 8 * group, 8)],
            inputs1.at[source],
            x_send,
            x_recv,
            (group, node),
        )

    def send_m(group, source, part):
        return send(
            stage1.at[pl.ds(8 * group + size1 * part, size1)],
            inputs1.at[8 + source, pl.ds(size1 * part, size1)],
            m_send,
            m_recv.at[part],
            (group, node),
        )

    def send_h(group, source, part):
        return send(
            parts1.at[group, pl.ds(size1 * part, size1)],
            table2.at[pl.ds(TILES + 8 * source + size1 * part, size1)],
            h_send,
            h_recv.at[part, source],
            (group, node),
        )

    def send_n(group, source, part):
        return send(
            stage2.at[pl.ds(8 * group + size2 * part, size2)],
            parts2.at[source, pl.ds(size2 * part, size2)],
            n_send,
            n_recv.at[part],
            (group, node),
        )

    others = range(GROUPS - 1)
    for i in others:
        send_x(far_first(i), z).start()
    closing.append(lambda: drain(inputs1.at[0:7], x_send))
    inputs1[z] = table1[pl.ds(TILES + 8 * z, 8)]

    for copy in small[:2]:
        copy.wait()

    loop(0, 16, lambda r: bit_copy(r).wait())

    def unpack_some(i):
        for u in range(8):
            unpack_row_tile(i * 8 + u, count_ref, bits, adj)

    loop(0, TILES // 8, unpack_some)

    to_up1.wait_recv()
    to_down1.wait_recv()

    place = iota((8, LANES), 1)
    exponents = place // 16 + 8 * ((place // 8) % 2)
    unscale = jnp.ones((8, LANES), F32)
    for bit in range(4):
        unscale = unscale * jnp.where((exponents >> bit) & 1 == 1, 0.5 ** (1 << bit), 1.0)

    def first_tile(t):
        values = picked_tiles(t, first_column, column_ref, table1)
        stacked = jnp.concatenate([values, jnp.ones((16, SLOTS * LANES), BF16)], axis=0)
        sums = lax.dot_general(stacked, adj[t], NT_DIMS, preferred_element_type=F32)
        inverse = unscale / jnp.maximum(sums[16:24] * unscale, 1.0)
        inv_degree[t] = inverse
        stage1[t] = (sums[:16] * inverse[:1]).astype(BF16)

    def aggregate(tile, send_part, part, size):
        count = 8 // size

        def some_groups(i):
            groups = [far_first(count * i + k) for k in range(count)]
            for group in groups:
                for u in range(size):
                    tile(group * 8 + size * part + u)
            for group in groups[:-1]:
                send_part(group, z, part).start()

            @pl.when(i < size - 1)
            def _():
                send_part(groups[-1], z, part).start()

        loop(0, size, some_groups)

    for part in range(FIRST_PARTS):
        aggregate(first_tile, send_m, part, size1)
    closing.append(lambda: drain(inputs1.at[8:15], m_send))

    def halo2(group, part, side, device):
        return send(
            table2.at[pl.ds(TILES + 8 * group + size1 * part, size1)],
            table2.at[pl.ds(2 * TILES * side + 8 * group + size1 * part, size1)],
            halo2_send.at[side],
            halo2_recv.at[side],
            (z, device),
        )

    def forward(group, part):
        halo2(group, part, 0, up).start()
        halo2(group, part, 1, down).start()

    for copy in small[2:]:
        copy.wait()

    eye = (iota((256, 256), 0) == iota((256, 256), 1)).astype(F32)
    for part, weight in enumerate((first_self, first_neighbor)):
        turned = lax.dot_general(eye.astype(BF16), weight[...], NT_DIMS, preferred_element_type=F32)
        w1[:, LANES * part : LANES * (part + 1)] = turned.astype(BF16)
    pick = (iota((CLS_PAD, CLS), 0) == iota((CLS_PAD, CLS), 1)).astype(F32)
    for part, weight in enumerate((second_self, second_neighbor)):
        padded = jnp.dot(pick.astype(BF16), weight[...], preferred_element_type=F32)
        w2[:, 256 * part : 256 * (part + 1)] = padded.astype(BF16)
    column1 = jnp.sum(jnp.where(eye > 0.5, first_bias[...], 0.0), axis=1, keepdims=True)
    b1[...] = jnp.broadcast_to(column1, (256, LANES))
    column2 = jnp.sum(jnp.where(pick > 0.5, second_bias[...], 0.0), axis=1, keepdims=True)
    column2 = jnp.where(iota((CLS_PAD, 1), 0) < CLS, column2, -1e30)
    b2[...] = jnp.broadcast_to(column2, (CLS_PAD, LANES))

    drain(inputs1.at[0:7], x_recv)
    for part in range(FIRST_PARTS):
        tiles = pl.ds(size1 * part, size1)
        inputs1[8 + z, tiles] = stage1[pl.ds(8 * z + size1 * part, size1)]
        drain(inputs1.at[8:15, tiles], m_recv.at[part])
        for u in range(size1 * part, size1 * (part + 1)):
            node_inputs = inputs1[:, u].reshape(256, LANES)
            total1 = jnp.dot(w1[...], node_inputs, preferred_element_type=F32)
            activated = jnp.maximum(total1 + b1[...], 0.0).astype(BF16)
            hidden[:, LANES * u : LANES * (u + 1)] = activated
            parts1[:, u] = activated.reshape(GROUPS, 32, LANES)
        for i in others:
            send_h(far_first(i), z, part).start()
        table2[pl.ds(TILES + 8 * z + size1 * part, size1)] = parts1[z, tiles]
        forward(z, part)
    closing.append(lambda: drain(parts1.at[0:7], h_send))

    for u in range(8):
        span = slice(LANES * u, LANES * (u + 1))
        moved = lax.dot_general(hidden[:, span], perm, NT_DIMS, preferred_element_type=F32)
        moved = moved.astype(BF16)
        second_inputs[0, :, span] = moved
        own_part = jnp.dot(w2[:, :256], moved, preferred_element_type=F32)
        own_scores[:, span] = own_part + b2[...]

    for part in range(FIRST_PARTS):

        def pass_on(i):
            group = far_first(i)
            send_h(z, group, part).wait_recv()
            forward(group, part)

        loop(0, GROUPS - 1, pass_on)

    for side in range(2):
        block = table2.at[pl.ds(2 * TILES * side, TILES)]
        closing.append(functools.partial(drain, block, halo2_send.at[side]))
        drain(block, halo2_recv.at[side])

    def second_tile(t):
        values = picked_tiles(t, first_column, column_ref, table2)
        sums = lax.dot_general(values, adj[t], NT_DIMS, preferred_element_type=F32)
        stage2[t] = (sums * inv_degree[t][:1]).astype(BF16)

    for part in range(SECOND_PARTS):
        aggregate(second_tile, send_n, part, size2)
    closing.append(lambda: drain(parts2.at[0:7], n_send))

    grad[CLS_PAD:256, :] = jnp.zeros((256 - CLS_PAD, GROUP), BF16)
    loss_lanes = jnp.zeros((1, LANES), F32)

    def gradient(part, half):
        span = slice(512 * half, 512 * (half + 1))
        product = lax.dot_general(
            grad[0:CLS_PAD, span],
            second_inputs[part, :, span],
            NT_DIMS,
            preferred_element_type=F32,
        )
        for side in range(2):
            place = pl.ds(pl.multiple_of(HALF * part + CLS_PAD * side, 8), CLS_PAD)
            values = product[:, LANES * side : LANES * (side + 1)]
            payload[place] = values if half == 0 else payload[place] + values

    for half in range(2):
        parts2[z, pl.ds(4 * half, 4)] = stage2[pl.ds(8 * z + 4 * half, 4)]
        drain(parts2.at[0:7, pl.ds(4 * half, 4)], n_recv.at[half])
        for u in range(4 * half, 4 * half + 4):
            span = slice(LANES * u, LANES * (u + 1))
            moved = lax.dot_general(
                parts2[:, u].reshape(256, LANES), perm, NT_DIMS, preferred_element_type=F32
            )
            moved = moved.astype(BF16)
            second_inputs[1, :, span] = moved
            score = own_scores[:, span] + jnp.dot(w2[:, 256:], moved, preferred_element_type=F32)
            logits_rows[:, :, span] = score[:CLS].reshape(CLS, 1, LANES)
            exponent = jnp.exp(score)
            class_total = jnp.sum(exponent, axis=0, keepdims=True)
            weight = train_mask[:, span].astype(F32)
            chosen = iota((CLS_PAD, LANES), 0) == labels[:, span]
            own_score = jnp.sum(jnp.where(chosen, score, 0.0), axis=0, keepdims=True)
            slope = exponent * (1.0 / class_total) - jnp.where(chosen, 1.0, 0.0)
            grad[0:CLS_PAD, span] = (slope * (weight * scale)).astype(BF16)
            loss_lanes = loss_lanes + (jnp.log(class_total) - own_score) * weight
        if half == 0:
            gradient(0, 0)
            gradient(1, 0)

    bias = lax.dot_general(
        jnp.ones((16, GROUP), BF16), grad[...], NT_DIMS, preferred_element_type=F32
    )
    loss = jnp.sum(loss_lanes, axis=1, keepdims=True) * (scale * scale)
    for part in range(2):
        start = HALF * part + 2 * CLS_PAD
        payload[start : start + 8] = bias[:8, :LANES]
        payload[start + 8 : start + 16] = bias[:8, LANES:]
        payload[start + 16 : start + 24] = jnp.broadcast_to(loss, (8, LANES))
        payload[start + 24 : start + 32] = jnp.zeros((8, LANES), F32)
    gradient(1 - core, 1)

    core_copy = send(
        payload.at[rows(1 - core, HALF), :], core_in, core_send.at[0], core_recv.at[0], (z, core_peer)
    )
    core_copy.start()
    closing.append(core_copy.wait_send)
    gradient(core, 1)
    logits_copy = pltpu.make_async_copy(logits_rows, logits_out, local_sem.at[3])
    logits_copy.start()
    closing.append(logits_copy.wait)
    core_copy.wait_recv()
    half_sum[...] = payload[rows(core, HALF), :] + core_in[...]

    def plane_copy(target, source):
        return send(
            half_sum.at[rows(target, PIECE), :],
            plane_in.at[source],
            plane_send,
            plane_recv,
            (z, target * 2 + core),
        )

    for peer in plane_peers:
        plane_copy(peer, plane).start()
    close()
    closing.append(lambda: drain(plane_in.at[0:15], plane_send))
    plane_in[plane] = half_sum[rows(plane, PIECE), :]
    drain(plane_in.at[0:15], plane_recv)
    line_in[z] = jnp.sum(plane_in[...], axis=0)

    def line_copy(target, source):
        return send(
            line_in.at[source], line_in.at[source], line_send, line_recv, (target, node)
        )

    for i in others:
        line_copy(far_first(i), z).start()
    close()
    closing.append(lambda: drain(line_in.at[0:7], line_send))
    drain(line_in.at[0:7], line_recv)
    total[rows(core * 16 + plane, PIECE), :] = jnp.sum(line_in[...], axis=0)

    def back_copy(target, source):
        part = total.at[rows(core * 16 + source, PIECE), :]
        return send(part, part, back_send, back_recv, (z, target * 2 + core))

    for peer in plane_peers:
        back_copy(peer, plane).start()
    close()
    pieces = total.at[0 : 15 * PIECE]
    drain(pieces, back_recv)
    closing.append(lambda: drain(pieces, back_send))

    def half_copy(which):
        part = total.at[rows(which, HALF), :]
        return send(part, part, core_send.at[1], core_recv.at[1], (z, core_peer))

    half_copy(core).start()
    closing.append(half_copy(core).wait_send)
    half_copy(1 - core).wait_recv()
    for part, held in enumerate((grad_self, grad_neighbor)):
        for side in range(2):
            start = HALF * part + CLS_PAD * side
            held[:, LANES * side : LANES * (side + 1)] = total[start : start + CLS]
    grad_bias[:, :LANES] = total[352:353]
    grad_bias[:, LANES:] = total[360:361, : CLS - LANES]
    loss_held[...] = total[368:369, :1]
    results = (
        (grad_self, grad_self_out),
        (grad_neighbor, grad_neighbor_out),
        (grad_bias, grad_bias_out),
        (loss_held, loss_out),
    )
    for i, (src, dst) in enumerate(results):
        copy = pltpu.make_async_copy(src, dst, small_sem.at[i])
        copy.start()
        closing.append(copy.wait)

    close()


def hand_over(*refs):
    sources, targets, places, arrive, leave = refs[:5], refs[5:10], refs[10:15], refs[15], refs[16]
    quarter = CLS // 4
    cuts = [(k, slice(None)) for k in range(1, 5)]
    cuts += [(0, slice(k * quarter, (k + 1) * quarter)) for k in range(4)]
    inward, outward = [], []
    for i, (k, cut) in enumerate(cuts):
        place = places[k].at[cut]
        inward.append(pltpu.make_async_copy(sources[k].at[cut], place, arrive.at[i]))
        outward.append(pltpu.make_async_copy(place, targets[k].at[cut], leave.at[i]))
    for copy in inward:
        copy.start()
    for first, second in zip(inward, outward):
        first.wait()
        second.start()
    for copy in outward:
        copy.wait()


def shards(
    features,
    tile_columns,
    tile_count,
    tile_bits,
    labels,
    train_mask,
    first_self,
    first_neighbor,
    first_bias,
    second_self,
    second_neighbor,
    second_bias,
):
    node_total = features.shape[2] * lax.axis_size("node")
    dma = pltpu.SemaphoreType.DMA
    anywhere = pl.BlockSpec(memory_space=pl.ANY)
    results = (
        jax.ShapeDtypeStruct((CLS, 1, GROUP), F32),
        jax.ShapeDtypeStruct((CLS, 256), F32),
        jax.ShapeDtypeStruct((CLS, 256), F32),
        jax.ShapeDtypeStruct((1, CLS), F32),
        jax.ShapeDtypeStruct((1, 1), F32),
    )
    held = pl.pallas_call(
        functools.partial(kernel, 1.0 / math.sqrt(node_total)),
        out_shape=results,
        in_specs=[anywhere] * 12,
        out_specs=(anywhere,) * 5,
        scratch_shapes=[
            pltpu.SMEM((SLOTS, TILES), jnp.int32),
            pltpu.SMEM((1, TILES), jnp.int32),
            pltpu.VMEM((1, GROUP), jnp.int32),
            pltpu.VMEM((1, GROUP), jnp.int32),
            pltpu.VMEM((LANES, 256), BF16),
            pltpu.VMEM((LANES, 256), BF16),
            pltpu.VMEM((1, 256), F32),
            pltpu.VMEM((CLS, 256), BF16),
            pltpu.VMEM((CLS, 256), BF16),
            pltpu.VMEM((1, CLS), F32),
            pltpu.VMEM((CLS, 256), F32),
            pltpu.VMEM((CLS, 256), F32),
            pltpu.VMEM((1, CLS), F32),
            pltpu.VMEM((1, 1), F32),
            pltpu.VMEM((16, BLOCK), BF16),
            pltpu.VMEM((TILES, 128, LANES), jnp.int32),
            pltpu.VMEM((TILES, LANES, SLOTS * LANES), BF16),
            pltpu.VMEM((3 * TILES, 16, LANES), BF16),
            pltpu.VMEM((TILES, 16, LANES), BF16),
            pltpu.VMEM((2 * GROUPS, 8, 16, LANES), BF16),
            pltpu.VMEM((3 * TILES, 32, LANES), BF16),
            pltpu.VMEM((TILES, 32, LANES), BF16),
            pltpu.VMEM((GROUPS, 8, 32, LANES), BF16),
            pltpu.VMEM((GROUPS, 8, 32, LANES), BF16),
            pltpu.VMEM((256, GROUP), BF16),
            pltpu.VMEM((TILES, 8, LANES), F32),
            pltpu.VMEM((2, 256, GROUP), BF16),
            pltpu.VMEM((CLS_PAD, GROUP), F32),
            pltpu.VMEM((256, 256), BF16),
            pltpu.VMEM((CLS_PAD, 512), BF16),
            pltpu.VMEM((256, LANES), F32),
            pltpu.VMEM((CLS_PAD, LANES), F32),
            pltpu.VMEM((CLS, 1, GROUP), F32),
            pltpu.VMEM((256, GROUP), BF16),
            pltpu.VMEM((2 * HALF, LANES), F32),
            pltpu.VMEM((HALF, LANES), F32),
            pltpu.VMEM((HALF, LANES), F32),
            pltpu.VMEM((16, PIECE, LANES), F32),
            pltpu.VMEM((GROUPS, PIECE, LANES), F32),
            pltpu.VMEM((2 * HALF, LANES), F32),
            dma((16,)),
            dma((10,)),
            dma((4,)),
            dma((2,)),
            dma((2,)),
            dma(()),
            dma(()),
            dma(()),
            dma((FIRST_PARTS,)),
            dma(()),
            dma((FIRST_PARTS, GROUPS)),
            dma((2,)),
            dma((2,)),
            dma(()),
            dma((SECOND_PARTS,)),
            dma((2,)),
            dma((2,)),
            dma(()),
            dma(()),
            dma(()),
            dma(()),
            dma(()),
            dma(()),
        ],
        compiler_params=pltpu.CompilerParams(
            collective_id=0, has_side_effects=True, vmem_limit_bytes=62 * 1024 * 1024
        ),
    )(
        features,
        tile_bits,
        tile_columns[0].T,
        tile_count,
        labels,
        train_mask,
        first_self,
        first_neighbor,
        first_bias[None],
        second_self.T,
        second_neighbor.T,
        second_bias[None],
    )
    logits, grad_self, grad_neighbor, grad_bias, loss = pl.pallas_call(
        hand_over,
        out_shape=results,
        in_specs=[anywhere] * 5,
        out_specs=(anywhere,) * 5,
        scratch_shapes=[pltpu.VMEM(r.shape, F32) for r in results] + [dma((8,)), dma((8,))],
        compiler_params=pltpu.CompilerParams(vmem_limit_bytes=62 * 1024 * 1024),
    )(*held)
    logits = jnp.transpose(logits, (1, 2, 0))
    return (logits, loss[0, 0], grad_self.T, grad_neighbor.T, grad_bias[0])


def solution(mesh):
    return jax.shard_map(
        shards,
        mesh=mesh,
        in_specs=(
            P("node", "feat", None),
            P("node", None, None),
            P("node", None),
            P("node", None, None, None),
            P("node", "feat"),
            P("node", "feat"),
            P(),
            P(),
            P(),
            P(),
            P(),
            P(),
        ),
        out_specs=(P("node", "feat", None), P(), P(), P(), P()),
        check_vma=False,
    )
```

```python
import functools
import math

import jax
import jax.numpy as jnp
from jax import lax
from jax.experimental import pallas as pl
from jax.experimental.pallas import tpu as pltpu
from jax.sharding import PartitionSpec as P

MESH = pl.DeviceIdType.MESH
F32 = jnp.float32
BF16 = jnp.bfloat16
NT_DIMS = (((1,), (1,)), ((), ()))
LANES = 128
SLOTS = 8
BLOCK = 8192
TILES = 64
GROUPS = 8
GROUP = 1024
CLS = 172
CLS_PAD = 176
PIECE = 24
FIRST_PARTS = 2
SECOND_PARTS = 2
HALF = 384


def iota(shape, axis):
    return lax.broadcasted_iota(jnp.int32, shape, axis)


def lanes(index, width=LANES):
    return pl.ds(pl.multiple_of(index * width, width), width)


def rows(index, height):
    return pl.ds(pl.multiple_of(index * height, height), height)


def loop(low, high, body):
    def step(i, carry):
        body(i)
        return carry

    lax.fori_loop(low, high, step, 0)


def permutation():
    j, p = iota((LANES, LANES), 0), iota((LANES, LANES), 1)
    return (j == 8 * (p % 16) + p // 16).astype(F32).astype(BF16)


def exchange_bits(words):
    group = iota(words.shape, 1) // 16
    for level, low_bits in ((0, 0x55555555), (1, 0x33333333), (2, 0x0F0F0F0F)):
        distance = 1 << level
        upper = ((group >> level) & 1) == 1
        keep = jnp.where(upper, ~jnp.int32(low_bits), jnp.int32(low_bits))
        from_above = pltpu.roll(words, LANES - 16 * distance, 1) << distance
        from_below = pltpu.roll(words, 16 * distance, 1) >> distance
        words = (words & keep) | (jnp.where(upper, from_below, from_above) & ~keep)
    return words


def unpack_row_tile(t, count_ref, bits, adj):
    limit = jnp.full((8, LANES), count_ref[0, t], jnp.int32)
    for pair in range(SLOTS // 2):
        packed = None
        for part in range(4):
            slot, half = 2 * pair + part // 2, part % 2
            piece = bits[t, pl.ds(64 * half + slot, 8, stride=8), :]
            piece = jnp.where(limit > slot, piece, 0) << (8 * part)
            packed = piece if packed is None else packed | piece
        packed = exchange_bits(packed)
        for side in range(2):
            slot = 2 * pair + side
            part = packed >> 16 if side else packed
            for low in range(8):
                first = part & (1 << low)
                second = part & (256 << low)
                both = jnp.concatenate([first, second], axis=0).astype(F32).astype(BF16)
                adj[t, 16 * low : 16 * low + 16, LANES * slot : LANES * (slot + 1)] = both


def picked_tiles(t, first_column, column_ref, table):
    parts = []
    for slot in range(SLOTS):
        index = jnp.clip(column_ref[slot, t] - first_column, 0, 3 * TILES - 1)
        parts.append(table[index])
    return jnp.concatenate(parts, axis=1)


def kernel(
    scale,
    features,
    bit_words,
    columns_in,
    count_in,
    labels_in,
    train_mask_in,
    first_self_in,
    first_neighbor_in,
    first_bias_in,
    second_self_in,
    second_neighbor_in,
    second_bias_in,
    logits_out,
    grad_self_out,
    grad_neighbor_out,
    grad_bias_out,
    loss_out,
    column_ref,
    count_ref,
    labels,
    train_mask,
    first_self,
    first_neighbor,
    first_bias,
    second_self,
    second_neighbor,
    second_bias,
    grad_self,
    grad_neighbor,
    grad_bias,
    loss_held,
    feats,
    bits,
    adj,
    table1,
    stage1,
    inputs1,
    table2,
    stage2,
    parts1,
    parts2,
    hidden,
    inv_degree,
    second_inputs,
    own_scores,
    w1,
    w2,
    b1,
    b2,
    logits_rows,
    grad,
    payload,
    core_in,
    half_sum,
    plane_in,
    line_in,
    total,
    bit_sem,
    small_sem,
    local_sem,
    halo1_send,
    halo1_recv,
    x_send,
    x_recv,
    m_send,
    m_recv,
    h_send,
    h_recv,
    halo2_send,
    halo2_recv,
    n_send,
    n_recv,
    core_send,
    core_recv,
    plane_send,
    plane_recv,
    line_send,
    line_recv,
    back_send,
    back_recv,
):
    z = lax.axis_index("feat")
    node = lax.axis_index("node")
    core = lax.rem(node, 2)
    plane = lax.div(node, 2)
    up = lax.rem(node + 1, 32)
    down = lax.rem(node + 31, 32)
    core_peer = plane * 2 + 1 - core
    first_column = (node - 1) * TILES

    def around(offset):
        return lax.rem(z + offset, GROUPS)

    def far_first(i):
        return around(4 + lax.div(i + 1, 2) * (1 - 2 * lax.rem(i, 2)))

    plane_x, plane_y = lax.div(plane, 4), lax.rem(plane, 4)
    plane_peers = [
        lax.rem(plane_x + dx, 4) * 4 + lax.rem(plane_y + dy, 4)
        for dx in (2, 1, 3, 0)
        for dy in (2, 1, 3, 0)
        if dx or dy
    ]

    def send(src, dst, send_sem, recv_sem, device):
        return pltpu.make_async_remote_copy(
            src_ref=src,
            dst_ref=dst,
            send_sem=send_sem,
            recv_sem=recv_sem,
            device_id=device,
            device_id_type=MESH,
        )

    def drain(ref, sem):
        send(ref, ref, sem, sem, (z, up)).wait_recv()

    closing = []

    def close():
        while closing:
            closing.pop(0)()

    barrier = pltpu.get_barrier_semaphore()

    def greet(device):
        pl.semaphore_signal(barrier, inc=1, device_id=device, device_id_type=MESH)

    loop(1, GROUPS, lambda o: greet((around(o), node)))
    for peer in plane_peers:
        greet((z, peer * 2 + core))
    greet((z, up))
    greet((z, down))

    feature_copy = pltpu.make_async_copy(features.at[0], feats, local_sem.at[0])
    feature_copy.start()

    def bit_copy(r):
        return pltpu.make_async_copy(
            bit_words.at[0, :, :, lanes(r)], bits.at[:, rows(r, 8), :], bit_sem.at[r]
        )

    loop(0, 16, lambda r: bit_copy(r).start())
    small = [
        pltpu.make_async_copy(src, dst, small_sem.at[i])
        for i, (src, dst) in enumerate(
            (
                (columns_in, column_ref),
                (count_in, count_ref),
                (first_self_in, first_self),
                (first_neighbor_in, first_neighbor),
                (first_bias_in, first_bias),
                (second_self_in, second_self),
                (second_neighbor_in, second_neighbor),
                (second_bias_in, second_bias),
                (labels_in, labels),
                (train_mask_in, train_mask),
            )
        )
    ]
    for copy in small:
        copy.start()

    perm = permutation()
    feature_copy.wait()

    def permute_features(i):
        for u in range(16):
            moved = jnp.dot(feats[:, lanes(16 * i + u)], perm, preferred_element_type=F32)
            table1[TILES + 16 * i + u] = moved.astype(BF16)

    loop(0, TILES // 16, permute_features)
    pl.semaphore_wait(barrier, 24)

    own1 = table1.at[pl.ds(TILES, TILES)]
    to_up1 = send(own1, table1.at[pl.ds(0, TILES)], halo1_send.at[0], halo1_recv.at[0], (z, up))
    to_down1 = send(own1, table1.at[pl.ds(2 * TILES, TILES)], halo1_send.at[1], halo1_recv.at[1], (z, down))
    to_up1.start()
    to_down1.start()
    closing.extend([to_up1.wait_send, to_down1.wait_send])
    size1, size2 = 8 // FIRST_PARTS, 8 // SECOND_PARTS

    def send_x(group, source):
        return send(
            table1.at[pl.ds(TILES + 8 * group, 8)],
            inputs1.at[source],
            x_send,
            x_recv,
            (group, node),
        )

    def send_m(group, source, part):
        return send(
            stage1.at[pl.ds(8 * group + size1 * part, size1)],
            inputs1.at[8 + source, pl.ds(size1 * part, size1)],
            m_send,
            m_recv.at[part],
            (group, node),
        )

    def send_h(group, source, part):
        return send(
            parts1.at[group, pl.ds(size1 * part, size1)],
            table2.at[pl.ds(TILES + 8 * source + size1 * part, size1)],
            h_send,
            h_recv.at[part, source],
            (group, node),
        )

    def send_n(group, source, part):
        return send(
            stage2.at[pl.ds(8 * group + size2 * part, size2)],
            parts2.at[source, pl.ds(size2 * part, size2)],
            n_send,
            n_recv.at[part],
            (group, node),
        )

    others = range(GROUPS - 1)
    for i in others:
        send_x(far_first(i), z).start()
    closing.append(lambda: drain(inputs1.at[0:7], x_send))
    inputs1[z] = table1[pl.ds(TILES + 8 * z, 8)]

    for copy in small[:2]:
        copy.wait()

    loop(0, 16, lambda r: bit_copy(r).wait())

    def unpack_some(i):
        for u in range(16):
            unpack_row_tile(i * 16 + u, count_ref, bits, adj)

    loop(0, TILES // 16, unpack_some)

    to_up1.wait_recv()
    to_down1.wait_recv()

    place = iota((8, LANES), 1)
    exponents = place // 16 + 8 * ((place // 8) % 2)
    unscale = jnp.ones((8, LANES), F32)
    for bit in range(4):
        unscale = unscale * jnp.where((exponents >> bit) & 1 == 1, 0.5 ** (1 << bit), 1.0)

    def first_tile(t):
        values = picked_tiles(t, first_column, column_ref, table1)
        stacked = jnp.concatenate([values, jnp.ones((16, SLOTS * LANES), BF16)], axis=0)
        sums = lax.dot_general(stacked, adj[t], NT_DIMS, preferred_element_type=F32)
        inverse = unscale / jnp.maximum(sums[16:24] * unscale, 1.0)
        inv_degree[t] = inverse
        stage1[t] = (sums[:16] * inverse[:1]).astype(BF16)

    def aggregate(tile, send_part, part, size):
        count = 8 // size

        def some_groups(i):
            groups = [far_first(count * i + k) for k in range(count)]
            for group in groups:
                for u in range(size):
                    tile(group * 8 + size * part + u)
            for group in groups[:-1]:
                send_part(group, z, part).start()

            @pl.when(i < size - 1)
            def _():
                send_part(groups[-1], z, part).start()

        loop(0, size, some_groups)

    for part in range(FIRST_PARTS):
        aggregate(first_tile, send_m, part, size1)
    closing.append(lambda: drain(inputs1.at[8:15], m_send))

    def halo2(group, part, side, device):
        return send(
            table2.at[pl.ds(TILES + 8 * group + size1 * part, size1)],
            table2.at[pl.ds(2 * TILES * side + 8 * group + size1 * part, size1)],
            halo2_send.at[side],
            halo2_recv.at[side],
            (z, device),
        )

    def forward(group, part):
        halo2(group, part, 0, up).start()
        halo2(group, part, 1, down).start()

    for copy in small[2:]:
        copy.wait()

    eye = (iota((256, 256), 0) == iota((256, 256), 1)).astype(F32)
    for part, weight in enumerate((first_self, first_neighbor)):
        turned = lax.dot_general(eye.astype(BF16), weight[...], NT_DIMS, preferred_element_type=F32)
        w1[:, LANES * part : LANES * (part + 1)] = turned.astype(BF16)
    pick = (iota((CLS_PAD, CLS), 0) == iota((CLS_PAD, CLS), 1)).astype(F32)
    for part, weight in enumerate((second_self, second_neighbor)):
        padded = jnp.dot(pick.astype(BF16), weight[...], preferred_element_type=F32)
        w2[:, 256 * part : 256 * (part + 1)] = padded.astype(BF16)
    column1 = jnp.sum(jnp.where(eye > 0.5, first_bias[...], 0.0), axis=1, keepdims=True)
    b1[...] = jnp.broadcast_to(column1, (256, LANES))
    column2 = jnp.sum(jnp.where(pick > 0.5, second_bias[...], 0.0), axis=1, keepdims=True)
    column2 = jnp.where(iota((CLS_PAD, 1), 0) < CLS, column2, -1e30)
    b2[...] = jnp.broadcast_to(column2, (CLS_PAD, LANES))

    drain(inputs1.at[0:7], x_recv)
    for part in range(FIRST_PARTS):
        tiles = pl.ds(size1 * part, size1)
        inputs1[8 + z, tiles] = stage1[pl.ds(8 * z + size1 * part, size1)]
        drain(inputs1.at[8:15, tiles], m_recv.at[part])
        for u in range(size1 * part, size1 * (part + 1)):
            node_inputs = inputs1[:, u].reshape(256, LANES)
            total1 = jnp.dot(w1[...], node_inputs, preferred_element_type=F32)
            activated = jnp.maximum(total1 + b1[...], 0.0).astype(BF16)
            hidden[:, LANES * u : LANES * (u + 1)] = activated
            parts1[:, u] = activated.reshape(GROUPS, 32, LANES)
        for i in others:
            send_h(far_first(i), z, part).start()
        table2[pl.ds(TILES + 8 * z + size1 * part, size1)] = parts1[z, tiles]
        forward(z, part)
    closing.append(lambda: drain(parts1.at[0:7], h_send))

    for u in range(8):
        span = slice(LANES * u, LANES * (u + 1))
        moved = lax.dot_general(hidden[:, span], perm, NT_DIMS, preferred_element_type=F32)
        moved = moved.astype(BF16)
        second_inputs[0, :, span] = moved
        own_part = jnp.dot(w2[:, :256], moved, preferred_element_type=F32)
        own_scores[:, span] = own_part + b2[...]

    for part in range(FIRST_PARTS):

        def pass_on(i):
            group = far_first(i)
            send_h(z, group, part).wait_recv()
            forward(group, part)

        loop(0, GROUPS - 1, pass_on)

    for side in range(2):
        block = table2.at[pl.ds(2 * TILES * side, TILES)]
        closing.append(functools.partial(drain, block, halo2_send.at[side]))
        drain(block, halo2_recv.at[side])

    def second_tile(t):
        values = picked_tiles(t, first_column, column_ref, table2)
        sums = lax.dot_general(values, adj[t], NT_DIMS, preferred_element_type=F32)
        stage2[t] = (sums * inv_degree[t][:1]).astype(BF16)

    for part in range(SECOND_PARTS):
        aggregate(second_tile, send_n, part, size2)
    closing.append(lambda: drain(parts2.at[0:7], n_send))

    grad[CLS_PAD:256, :] = jnp.zeros((256 - CLS_PAD, GROUP), BF16)
    loss_lanes = jnp.zeros((1, LANES), F32)

    def gradient(part, half):
        span = slice(512 * half, 512 * (half + 1))
        product = lax.dot_general(
            grad[0:CLS_PAD, span],
            second_inputs[part, :, span],
            NT_DIMS,
            preferred_element_type=F32,
        )
        for side in range(2):
            place = pl.ds(pl.multiple_of(HALF * part + CLS_PAD * side, 8), CLS_PAD)
            values = product[:, LANES * side : LANES * (side + 1)]
            payload[place] = values if half == 0 else payload[place] + values

    for half in range(2):
        parts2[z, pl.ds(4 * half, 4)] = stage2[pl.ds(8 * z + 4 * half, 4)]
        drain(parts2.at[0:7, pl.ds(4 * half, 4)], n_recv.at[half])
        for u in range(4 * half, 4 * half + 4):
            span = slice(LANES * u, LANES * (u + 1))
            moved = lax.dot_general(
                parts2[:, u].reshape(256, LANES), perm, NT_DIMS, preferred_element_type=F32
            )
            moved = moved.astype(BF16)
            second_inputs[1, :, span] = moved
            score = own_scores[:, span] + jnp.dot(w2[:, 256:], moved, preferred_element_type=F32)
            logits_rows[:, :, span] = score[:CLS].reshape(CLS, 1, LANES)
            exponent = jnp.exp(score)
            class_total = jnp.sum(exponent, axis=0, keepdims=True)
            weight = train_mask[:, span].astype(F32)
            chosen = iota((CLS_PAD, LANES), 0) == labels[:, span]
            own_score = jnp.sum(jnp.where(chosen, score, 0.0), axis=0, keepdims=True)
            slope = exponent * (1.0 / class_total) - jnp.where(chosen, 1.0, 0.0)
            grad[0:CLS_PAD, span] = (slope * (weight * scale)).astype(BF16)
            loss_lanes = loss_lanes + (jnp.log(class_total) - own_score) * weight
        if half == 0:
            gradient(0, 0)
            gradient(1, 0)

    bias = lax.dot_general(
        jnp.ones((16, GROUP), BF16), grad[...], NT_DIMS, preferred_element_type=F32
    )
    loss = jnp.sum(loss_lanes, axis=1, keepdims=True) * (scale * scale)
    for part in range(2):
        start = HALF * part + 2 * CLS_PAD
        payload[start : start + 8] = bias[:8, :LANES]
        payload[start + 8 : start + 16] = bias[:8, LANES:]
        payload[start + 16 : start + 24] = jnp.broadcast_to(loss, (8, LANES))
        payload[start + 24 : start + 32] = jnp.zeros((8, LANES), F32)
    gradient(1 - core, 1)

    core_copy = send(
        payload.at[rows(1 - core, HALF), :], core_in, core_send.at[0], core_recv.at[0], (z, core_peer)
    )
    core_copy.start()
    closing.append(core_copy.wait_send)
    gradient(core, 1)
    logits_copy = pltpu.make_async_copy(logits_rows, logits_out, local_sem.at[3])
    logits_copy.start()
    closing.append(logits_copy.wait)
    core_copy.wait_recv()
    half_sum[...] = payload[rows(core, HALF), :] + core_in[...]

    def plane_copy(target, source):
        return send(
            half_sum.at[rows(target, PIECE), :],
            plane_in.at[source],
            plane_send,
            plane_recv,
            (z, target * 2 + core),
        )

    for peer in plane_peers:
        plane_copy(peer, plane).start()
    close()
    closing.append(lambda: drain(plane_in.at[0:15], plane_send))
    plane_in[plane] = half_sum[rows(plane, PIECE), :]
    drain(plane_in.at[0:15], plane_recv)
    line_in[z] = jnp.sum(plane_in[...], axis=0)

    def line_copy(target, source):
        return send(
            line_in.at[source], line_in.at[source], line_send, line_recv, (target, node)
        )

    for i in others:
        line_copy(far_first(i), z).start()
    close()
    closing.append(lambda: drain(line_in.at[0:7], line_send))
    drain(line_in.at[0:7], line_recv)
    total[rows(core * 16 + plane, PIECE), :] = jnp.sum(line_in[...], axis=0)

    def back_copy(target, source):
        part = total.at[rows(core * 16 + source, PIECE), :]
        return send(part, part, back_send, back_recv, (z, target * 2 + core))

    for peer in plane_peers:
        back_copy(peer, plane).start()
    close()
    pieces = total.at[0 : 15 * PIECE]
    drain(pieces, back_recv)
    closing.append(lambda: drain(pieces, back_send))

    def half_copy(which):
        part = total.at[rows(which, HALF), :]
        return send(part, part, core_send.at[1], core_recv.at[1], (z, core_peer))

    half_copy(core).start()
    closing.append(half_copy(core).wait_send)
    half_copy(1 - core).wait_recv()
    for part, held in enumerate((grad_self, grad_neighbor)):
        for side in range(2):
            start = HALF * part + CLS_PAD * side
            held[:, LANES * side : LANES * (side + 1)] = total[start : start + CLS]
    grad_bias[:, :LANES] = total[352:353]
    grad_bias[:, LANES:] = total[360:361, : CLS - LANES]
    loss_held[...] = total[368:369, :1]
    results = (
        (grad_self, grad_self_out),
        (grad_neighbor, grad_neighbor_out),
        (grad_bias, grad_bias_out),
        (loss_held, loss_out),
    )
    for i, (src, dst) in enumerate(results):
        copy = pltpu.make_async_copy(src, dst, small_sem.at[i])
        copy.start()
        closing.append(copy.wait)

    close()


def hand_over(*refs):
    sources, targets, places, arrive, leave = refs[:5], refs[5:10], refs[10:15], refs[15], refs[16]
    quarter = CLS // 4
    cuts = [(k, slice(None)) for k in range(1, 5)]
    cuts += [(0, slice(k * quarter, (k + 1) * quarter)) for k in range(4)]
    inward, outward = [], []
    for i, (k, cut) in enumerate(cuts):
        place = places[k].at[cut]
        inward.append(pltpu.make_async_copy(sources[k].at[cut], place, arrive.at[i]))
        outward.append(pltpu.make_async_copy(place, targets[k].at[cut], leave.at[i]))
    for copy in inward:
        copy.start()
    for first, second in zip(inward, outward):
        first.wait()
        second.start()
    for copy in outward:
        copy.wait()


def shards(
    features,
    tile_columns,
    tile_count,
    tile_bits,
    labels,
    train_mask,
    first_self,
    first_neighbor,
    first_bias,
    second_self,
    second_neighbor,
    second_bias,
):
    node_total = features.shape[2] * lax.axis_size("node")
    dma = pltpu.SemaphoreType.DMA
    anywhere = pl.BlockSpec(memory_space=pl.ANY)
    results = (
        jax.ShapeDtypeStruct((CLS, 1, GROUP), F32),
        jax.ShapeDtypeStruct((CLS, 256), F32),
        jax.ShapeDtypeStruct((CLS, 256), F32),
        jax.ShapeDtypeStruct((1, CLS), F32),
        jax.ShapeDtypeStruct((1, 1), F32),
    )
    held = pl.pallas_call(
        functools.partial(kernel, 1.0 / math.sqrt(node_total)),
        out_shape=results,
        in_specs=[anywhere] * 12,
        out_specs=(anywhere,) * 5,
        scratch_shapes=[
            pltpu.SMEM((SLOTS, TILES), jnp.int32),
            pltpu.SMEM((1, TILES), jnp.int32),
            pltpu.VMEM((1, GROUP), jnp.int32),
            pltpu.VMEM((1, GROUP), jnp.int32),
            pltpu.VMEM((LANES, 256), BF16),
            pltpu.VMEM((LANES, 256), BF16),
            pltpu.VMEM((1, 256), F32),
            pltpu.VMEM((CLS, 256), BF16),
            pltpu.VMEM((CLS, 256), BF16),
            pltpu.VMEM((1, CLS), F32),
            pltpu.VMEM((CLS, 256), F32),
            pltpu.VMEM((CLS, 256), F32),
            pltpu.VMEM((1, CLS), F32),
            pltpu.VMEM((1, 1), F32),
            pltpu.VMEM((16, BLOCK), BF16),
            pltpu.VMEM((TILES, 128, LANES), jnp.int32),
            pltpu.VMEM((TILES, LANES, SLOTS * LANES), BF16),
            pltpu.VMEM((3 * TILES, 16, LANES), BF16),
            pltpu.VMEM((TILES, 16, LANES), BF16),
            pltpu.VMEM((2 * GROUPS, 8, 16, LANES), BF16),
            pltpu.VMEM((3 * TILES, 32, LANES), BF16),
            pltpu.VMEM((TILES, 32, LANES), BF16),
            pltpu.VMEM((GROUPS, 8, 32, LANES), BF16),
            pltpu.VMEM((GROUPS, 8, 32, LANES), BF16),
            pltpu.VMEM((256, GROUP), BF16),
            pltpu.VMEM((TILES, 8, LANES), F32),
            pltpu.VMEM((2, 256, GROUP), BF16),
            pltpu.VMEM((CLS_PAD, GROUP), F32),
            pltpu.VMEM((256, 256), BF16),
            pltpu.VMEM((CLS_PAD, 512), BF16),
            pltpu.VMEM((256, LANES), F32),
            pltpu.VMEM((CLS_PAD, LANES), F32),
            pltpu.VMEM((CLS, 1, GROUP), F32),
            pltpu.VMEM((256, GROUP), BF16),
            pltpu.VMEM((2 * HALF, LANES), F32),
            pltpu.VMEM((HALF, LANES), F32),
            pltpu.VMEM((HALF, LANES), F32),
            pltpu.VMEM((16, PIECE, LANES), F32),
            pltpu.VMEM((GROUPS, PIECE, LANES), F32),
            pltpu.VMEM((2 * HALF, LANES), F32),
            dma((16,)),
            dma((10,)),
            dma((4,)),
            dma((2,)),
            dma((2,)),
            dma(()),
            dma(()),
            dma(()),
            dma((FIRST_PARTS,)),
            dma(()),
            dma((FIRST_PARTS, GROUPS)),
            dma((2,)),
            dma((2,)),
            dma(()),
            dma((SECOND_PARTS,)),
            dma((2,)),
            dma((2,)),
            dma(()),
            dma(()),
            dma(()),
            dma(()),
            dma(()),
            dma(()),
        ],
        compiler_params=pltpu.CompilerParams(
            collective_id=0, has_side_effects=True, vmem_limit_bytes=62 * 1024 * 1024
        ),
    )(
        features,
        tile_bits,
        tile_columns[0].T,
        tile_count,
        labels,
        train_mask,
        first_self,
        first_neighbor,
        first_bias[None],
        second_self.T,
        second_neighbor.T,
        second_bias[None],
    )
    logits, grad_self, grad_neighbor, grad_bias, loss = pl.pallas_call(
        hand_over,
        out_shape=results,
        in_specs=[anywhere] * 5,
        out_specs=(anywhere,) * 5,
        scratch_shapes=[pltpu.VMEM(r.shape, F32) for r in results] + [dma((8,)), dma((8,))],
        compiler_params=pltpu.CompilerParams(vmem_limit_bytes=62 * 1024 * 1024),
    )(*held)
    logits = jnp.transpose(logits, (1, 2, 0))
    return (logits, loss[0, 0], grad_self.T, grad_neighbor.T, grad_bias[0])


def solution(mesh):
    return jax.shard_map(
        shards,
        mesh=mesh,
        in_specs=(
            P("node", "feat", None),
            P("node", None, None),
            P("node", None),
            P("node", None, None, None),
            P("node", "feat"),
            P("node", "feat"),
            P(),
            P(),
            P(),
            P(),
            P(),
            P(),
        ),
        out_specs=(P("node", "feat", None), P(), P(), P(), P()),
        check_vma=False,
    )
```
